32 devices in a mesh: rows: 8 (over y, x, core), cols: 4 (over z).
Axes of the slice: x: 2, y: 2, z: 4, core: 2. Of those that a mesh axis runs over, the one named last changes fastest.
Arguments:
- tiles: float32 [8, 32, 128, 128], P('rows', 'cols'), may hold values from -0.1875 to 0.1875
- tile_rows: int32 [8, 32], P('rows', 'cols'), may hold values from 0 to 1
- tile_cols: int32 [8, 32], P('rows', 'cols'), may hold values from 0 to 15
- counts: int32 [8, 4], P('rows', 'cols'), may hold values from 1 to 8, as said below
- scaling: float32 [8192], P('cols'), may hold values from 0.1 to 10
Outputs:
- normal: float32 [2048, 2048], P('rows', 'cols')
The draws below stay inside these ranges and needn't reach their ends.
Inputs may be any that keep to these rules, and one draw needn't show every extreme that they name: `counts`: in every draw some panels have all 8 slots live in every column group; the others have at most 5.
All inputs are finite; a program needn't handle non-finite values.
Results may differ from the reference program's by a relative error of at most 0.0003.
Values sent between devices are 32-bit elements; how exact they have to be, the bound alone decides.
No kernel may reach another device: no remote copies, remote signals or barrier semaphores. Data moves between devices by JAX's collectives and lax.ppermute only.
A program may use at most 192 MiB of HBM per device.

```python
import math
import jax
import jax.numpy as jnp
from jax import lax

TB = 128
RB = 2
CB_DEV = 16
KT = 8
PANELS = 8
GROUPS = 4
NCON = 2048
NVAR = 8192


def draw_counts(key, part):
    first_key, second_key, third_key = jax.random.split(key, 3)
    base_counts = jax.random.randint(first_key, (PANELS, GROUPS), 1, KT // 2 + 2)
    linking = jax.random.randint(second_key, (PANELS,), 0, 8) == 0
    forced = jax.random.randint(third_key, (), 0, PANELS)
    linking = linking | (jnp.arange(PANELS) == forced)
    return jnp.where(linking[:, None], KT, base_counts).astype(jnp.int32)


def plant(array, own_key, low, high):
    longest = array.shape.index(max(array.shape))
    spots = []
    for shift in (0, 1):
        where = [jax.random.randint(jax.random.fold_in(own_key, axis), (), 0, length) for axis, length in enumerate(array.shape)]
        where[longest] = (where[longest] + shift) % array.shape[longest]
        spots.append(tuple(where))
    return array.at[spots[0]].set(low).at[spots[1]].set(high)


def block_levels(stream_key, dims, pieces, smallest, top_value):
    def one(position, shards_of):
        steps = jax.random.uniform(jax.random.fold_in(jax.random.fold_in(stream_key, 6), position), (shards_of,), jnp.float32, smallest / len(pieces), top_value / len(pieces))
        return jnp.repeat(jnp.exp(steps), dims[position] // shards_of).reshape((-1,) + (1,) * (len(dims) - position - 1))

    loudness = one(*pieces[0])
    for cut in pieces[1:]:
        loudness = loudness * one(*cut)
    return loudness


def normal_values(rng, extent, scale, limit, shards=(), kind=jnp.bfloat16):
    drawn = jax.random.normal(rng, extent, jnp.float32) * scale
    if len(shards) > 0:
        drawn = block_levels(rng, extent, shards, -0.22, 0.18) * drawn
    return jnp.clip(drawn, min=-limit, max=limit).astype(kind)


def setup_inputs(seed: int = 0) -> dict:
    keys = jax.random.split(jax.random.key(seed), 6)
    return {
        "tiles": normal_values(keys[0], (PANELS, GROUPS * KT, TB, TB), (TB * KT) ** -0.5, 0.1875, ((0, 8), (1, 4)), jnp.float32),
        "tile_rows": plant(jax.random.randint(keys[1], (PANELS, GROUPS * KT), 0, RB), jax.random.fold_in(keys[1], 1), 0, RB - 1).astype(jnp.int32),
        "tile_cols": plant(jax.random.randint(keys[2], (PANELS, GROUPS * KT), 0, CB_DEV), jax.random.fold_in(keys[2], 1), 0, CB_DEV - 1).astype(jnp.int32),
        "counts": draw_counts(jax.random.fold_in(keys[5], 71), 0),
        "scaling": jnp.clip(jnp.exp(math.log(10.0) - 4.6051702 * jax.random.uniform(keys[4], (NVAR,), jnp.float32) ** block_levels(keys[4], (NVAR,), ((0, 4),), -0.2, 0.2)), 0.1, 10.0),
    }


def densify(tile_set, row_ids, col_ids, live_mask, scale_set):
    hit_col = (col_ids[:, None] == jnp.arange(CB_DEV, dtype=jnp.int32)[None, :]).astype(jnp.float32) * live_mask[:, None]
    hit_row = (row_ids[:, None] == jnp.arange(RB, dtype=jnp.int32)[None, :]).astype(jnp.float32)
    placed = jnp.einsum('kj,kr,kab->jrab', hit_col, hit_row, tile_set, precision=lax.Precision.HIGHEST)
    placed = placed * scale_set[:, None, None, :]
    return placed.reshape(CB_DEV, RB * TB, TB)


def reference(tiles, tile_rows, tile_cols, counts, scaling):
    def group_term(running, group):
        group_tiles = lax.dynamic_slice_in_dim(tiles, group * KT, KT, 1)
        group_rows = lax.dynamic_slice_in_dim(tile_rows, group * KT, KT, 1)
        group_cols = lax.dynamic_slice_in_dim(tile_cols, group * KT, KT, 1)
        group_count = lax.dynamic_slice_in_dim(counts, group, 1, 1)[:, 0]
        group_scale = lax.dynamic_slice_in_dim(scaling, group * CB_DEV * TB, CB_DEV * TB).reshape(CB_DEV, TB)
        live_mask = (jnp.arange(KT, dtype=jnp.int32)[None, :] < group_count[:, None]).astype(jnp.float32)
        blocked = jax.vmap(densify, in_axes=(0, 0, 0, 0, None))(group_tiles, group_rows, group_cols, live_mask, group_scale)

        def column_panel(inputs):
            far_tiles, far_rows, far_cols, far_live = inputs
            picked = jnp.take(blocked, far_cols, axis=1)
            product = jnp.einsum('pkac,kbc->pkab', picked, far_tiles, precision=lax.Precision.HIGHEST)
            hit_row = (far_rows[:, None] == jnp.arange(RB, dtype=jnp.int32)[None, :]).astype(jnp.float32) * far_live[:, None]
            placed = jnp.einsum('kr,pkab->parb', hit_row, product, precision=lax.Precision.HIGHEST)
            return placed.reshape(PANELS, RB * TB, RB * TB)

        columns = lax.map(column_panel, (group_tiles, group_rows, group_cols, live_mask))
        term = jnp.transpose(columns, (1, 2, 0, 3)).reshape(NCON, NCON)
        return running + term, None

    start = jnp.zeros((NCON, NCON), jnp.float32)
    normal, _ = lax.scan(group_term, start, jnp.arange(GROUPS, dtype=jnp.int32))
    return normal
```

```python
import functools

import jax
import jax.numpy as jnp
from jax import lax
from jax.experimental import pallas as pl
from jax.experimental.pallas import tpu as pltpu
from jax.sharding import PartitionSpec as P

TB = 128
RB = 2
CB_DEV = 16
PANEL = RB * TB
META = 8
CUTS = 2
AXES = ("rows", "cols")
VMEM_LIMIT = 40 * 1024 * 1024
VSPEC = pl.BlockSpec(memory_space=pltpu.VMEM)
SSPEC = pl.BlockSpec(memory_space=pltpu.SMEM)


def params():
    return pltpu.CompilerParams(vmem_limit_bytes=VMEM_LIMIT)


def cost(flops, nbytes):
    return pl.CostEstimate(flops=flops, bytes_accessed=nbytes, transcendentals=0)


def pack_kernel(slots, cut_rows, rows_ref, cols_ref, counts_ref, tiles_ref, scale_ref, *out_refs):
    lane = lax.broadcasted_iota(jnp.int32, (META, TB), 1)
    codes = jnp.full((META, TB), -1.0, jnp.float32)
    count = counts_ref[0, 0]
    for slot in range(slots):
        live = slot < count
        row = rows_ref[0, slot]
        col = cols_ref[0, slot]
        factor = jnp.where(live, jnp.sqrt(scale_ref[pl.ds(col, 1), :]), 0.0)
        for cut, out_ref in enumerate(out_refs):
            out_ref[slot * cut_rows : (slot + 1) * cut_rows, :] = (
                tiles_ref[0, slot, cut * cut_rows : (cut + 1) * cut_rows, :] * factor
            )
        code = jnp.where(live, col * RB + row, -1).astype(jnp.float32)
        codes = jnp.where(lane == slot, code, codes)
    for out_ref in out_refs:
        out_ref[slots * cut_rows :, :] = codes


def pack(tiles, tile_rows, tile_cols, counts, scaling, cuts):
    slots = tiles.shape[1]
    cut_rows = TB // cuts
    shape = jax.ShapeDtypeStruct((slots * cut_rows + META, TB), jnp.float32)
    return pl.pallas_call(
        functools.partial(pack_kernel, slots, cut_rows),
        out_shape=[shape] * cuts,
        in_specs=[SSPEC] * 3 + [VSPEC] * 2,
        out_specs=[VSPEC] * cuts,
        compiler_params=params(),
        cost_estimate=cost(slots * TB * TB, 2 * slots * TB * TB * 4),
        name="pack",
    )(tile_rows, tile_cols, counts, tiles, scaling.reshape(CB_DEV, TB))


def read_codes(piece_ref, base, code_ref, sem):
    copy = pltpu.make_async_copy(piece_ref.at[pl.ds(base, META)], code_ref, sem)
    copy.start()
    copy.wait()


def spread_kernel(slots, cut_rows, cuts, *refs):
    pieces = refs[: 2 * cuts]
    dense_ref, code_ref, sem = refs[2 * cuts :]
    dense_ref[...] = jnp.zeros_like(dense_ref)
    for side in range(2):
        own = pieces[side * cuts : (side + 1) * cuts]
        read_codes(own[0], slots * cut_rows, code_ref, sem)
        for slot in range(slots):
            code = code_ref[0, slot].astype(jnp.int32)

            @pl.when(code >= 0)
            def _(code=code, own=own, slot=slot, side=side):
                col = code >> 1
                start = pl.multiple_of(side * PANEL + (code & 1) * TB, TB)
                for cut, piece_ref in enumerate(own):
                    place = pl.ds(start + cut * cut_rows, cut_rows)
                    dense_ref[col, place, :] += piece_ref[slot * cut_rows : (slot + 1) * cut_rows, :]


def spread(own, other, slots):
    cuts = len(own)
    cut_rows = TB // cuts
    return pl.pallas_call(
        functools.partial(spread_kernel, slots, cut_rows, cuts),
        out_shape=jax.ShapeDtypeStruct((CB_DEV, 2 * PANEL, TB), jnp.float32),
        in_specs=[VSPEC] * (2 * cuts),
        out_specs=VSPEC,
        scratch_shapes=[pltpu.SMEM((META, TB), jnp.float32), pltpu.SemaphoreType.DMA],
        compiler_params=params(),
        cost_estimate=cost(1 << 20, CB_DEV * 2 * PANEL * TB * 8),
        name="spread",
    )(*own, *other)


def split(x):
    high = x.astype(jnp.bfloat16)
    low = (x - high.astype(jnp.float32)).astype(jnp.bfloat16)
    return high, low


def nt_dot(a, b):
    return lax.dot_general(a, b, (((1,), (1,)), ((), ())), preferred_element_type=jnp.float32)


def add_products(slots, cut_rows, flag_ref, dense_ref, piece_refs, acc_ref, code_ref, sem):
    for which, piece_ref in enumerate(piece_refs):
        chunk = flag_ref[0] if which == 0 else 1 - flag_ref[0]
        read_codes(piece_ref, slots * cut_rows, code_ref, sem)
        for slot in range(slots):
            code = code_ref[0, slot].astype(jnp.int32)

            @pl.when(code >= 0)
            def _(code=code, piece_ref=piece_ref, slot=slot, chunk=chunk):
                left_high, left_low = split(dense_ref[code >> 1])
                high, low = split(piece_ref[slot * cut_rows : (slot + 1) * cut_rows, :])
                acc_ref[chunk, code & 1] += (
                    nt_dot(left_high, high) + nt_dot(left_high, low) + nt_dot(left_low, high)
                )


def first_kernel(slots, cut_rows, cuts, flag_ref, dense_ref, *refs):
    pieces = refs[: 2 * cuts]
    acc_refs = refs[2 * cuts : 3 * cuts]
    code_ref, sem = refs[3 * cuts :]
    for cut in range(cuts):
        acc_refs[cut][...] = jnp.zeros_like(acc_refs[cut])
        add_products(
            slots, cut_rows, flag_ref, dense_ref, (pieces[cut], pieces[cuts + cut]), acc_refs[cut], code_ref, sem
        )


def first(flag, dense, right_a, right_b, slots):
    cuts = len(right_a)
    cut_rows = TB // cuts
    shape = jax.ShapeDtypeStruct((2, RB, 2 * PANEL, cut_rows), jnp.float32)
    return pl.pallas_call(
        functools.partial(first_kernel, slots, cut_rows, cuts),
        out_shape=[shape] * cuts,
        in_specs=[SSPEC] + [VSPEC] * (1 + 2 * cuts),
        out_specs=[VSPEC] * cuts,
        scratch_shapes=[pltpu.SMEM((META, TB), jnp.float32), pltpu.SemaphoreType.DMA],
        compiler_params=params(),
        cost_estimate=cost(2 * slots * 6 * 2 * PANEL * TB * TB, CB_DEV * 2 * PANEL * TB * 8),
        name="first",
    )(flag, dense, *right_a, *right_b)


def second_kernel(slots, cut_rows, flag_ref, dense_ref, acc_in_ref, a_ref, b_ref, *refs):
    out_refs = refs[:4]
    acc_ref, code_ref, sem = refs[4:]
    acc_ref[...] = acc_in_ref[...]
    add_products(slots, cut_rows, flag_ref, dense_ref, (a_ref, b_ref), acc_ref, code_ref, sem)
    for chunk in range(2):
        for side in range(2):
            part = [acc_ref[chunk, block, side * PANEL : (side + 1) * PANEL, :] for block in range(RB)]
            out_refs[2 * chunk + side][...] = jnp.concatenate(part, axis=1)


def second(flag, dense, acc, piece_a, piece_b, slots):
    cut_rows = acc.shape[-1]
    shape = jax.ShapeDtypeStruct((PANEL, RB * cut_rows), jnp.float32)
    return pl.pallas_call(
        functools.partial(second_kernel, slots, cut_rows),
        out_shape=[shape] * 4,
        in_specs=[SSPEC] + [VSPEC] * 4,
        out_specs=[VSPEC] * 4,
        scratch_shapes=[
            pltpu.VMEM(acc.shape, jnp.float32),
            pltpu.SMEM((META, TB), jnp.float32),
            pltpu.SemaphoreType.DMA,
        ],
        compiler_params=params(),
        cost_estimate=cost(slots * 12 * 2 * PANEL * TB * cut_rows, CB_DEV * 2 * PANEL * TB * 4),
        name="second",
    )(flag, dense, acc, piece_a, piece_b)


def join_kernel(cuts, cut_rows, core_ref, *refs):
    out_ref = refs[-1]
    core = core_ref[0]
    for side in range(2):
        halves = [refs[side * cuts + cut][...] + refs[(2 + side) * cuts + cut][...] for cut in range(cuts)]
        for block in range(RB):
            part = [half[:, block * cut_rows : (block + 1) * cut_rows] for half in halves]
            panel = core if side == 0 else 1 - core
            start = pl.multiple_of(panel * PANEL + block * TB, TB)
            out_ref[:, pl.ds(start, TB)] = part[0] if cuts == 1 else jnp.concatenate(part, axis=1)


def join(core, near_same, near_cross, far_same, far_cross):
    cuts = len(near_same)
    return pl.pallas_call(
        functools.partial(join_kernel, cuts, TB // cuts),
        out_shape=jax.ShapeDtypeStruct((PANEL, 2 * PANEL), jnp.float32),
        in_specs=[SSPEC] + [VSPEC] * (4 * cuts),
        out_specs=VSPEC,
        compiler_params=params(),
        cost_estimate=cost(PANEL * 2 * PANEL, PANEL * 2 * PANEL * 12),
        name="join",
    )(core, *near_same, *near_cross, *far_same, *far_cross)


def pairs(place):
    out = []
    for row in range(8):
        for col in range(4):
            chip, core, plane = place(row >> 1, row & 1, col)
            out.append((row * 4 + col, (chip * 2 + core) * 4 + plane))
    return out


def outer(plane):
    return plane in (0, 3)


SWAP = pairs(lambda k, i, p: (k, 1 - i, p))
NEXT = pairs(lambda k, i, p: (k, i, p ^ 1))
SEND_A = pairs(lambda k, i, p: (k if outer(p) else k ^ 1, i, p))
SEND_B = pairs(lambda k, i, p: (k ^ 3 if outer(p) else k ^ 2, i, p))
NEAR = pairs(lambda k, i, p: (k, i, p if outer(k) else p ^ 1))
FAR = pairs(lambda k, i, p: (k, i, p ^ 3 if outer(k) else p ^ 2))
NEAR_CROSS = pairs(lambda k, i, p: (k, 1 - i, p if outer(k) else p ^ 1))
FAR_CROSS = pairs(lambda k, i, p: (k, 1 - i, p ^ 3 if outer(k) else p ^ 2))


def send(pieces, perm):
    return [lax.ppermute(piece, AXES, perm) for piece in pieces]


def per_device(tiles, tile_rows, tile_cols, counts, scaling):
    slots = tiles.shape[1]
    row = lax.axis_index("rows")
    plane = lax.axis_index("cols")
    chip, core = row >> 1, row & 1
    chip_outer = (chip == 0) | (chip == 3)
    plane_outer = (plane == 0) | (plane == 3)
    chunk_a = jnp.where(plane_outer, chip, chip ^ 1)
    near = jnp.where(chip_outer, plane, plane ^ 1)
    flag = jnp.where(chunk_a == near, 0, 1).astype(jnp.int32).reshape(1)

    own = pack(tiles, tile_rows, tile_cols, counts, scaling, CUTS)
    next_own = send(own, NEXT)
    own_a = send(own, SEND_A)
    own_b = send(own, SEND_B)
    own_other = send(own, SWAP)
    next_a = send(next_own, SEND_A)
    next_b = send(next_own, SEND_B)
    next_other = send(next_own, SWAP)
    own_dense = spread(own, own_other, slots)
    accs = first(flag, own_dense, own_a, own_b, slots)
    next_dense = spread(next_own, next_other, slots)
    near_same, near_cross, far_same, far_cross = [], [], [], []
    for cut in range(CUTS):
        results = second(flag, next_dense, accs[cut], next_a[cut], next_b[cut], slots)
        far_same.append(lax.ppermute(results[2], AXES, FAR))
        far_cross.append(lax.ppermute(results[3], AXES, FAR_CROSS))
        near_same.append(lax.ppermute(results[0], AXES, NEAR))
        near_cross.append(lax.ppermute(results[1], AXES, NEAR_CROSS))
    return join(core.astype(jnp.int32).reshape(1), near_same, near_cross, far_same, far_cross)


def densify(tile_set, row_ids, col_ids, live_mask, scale_set, block_count):
    placed = jnp.zeros((block_count, RB, TB, TB), jnp.float32)
    placed = placed.at[col_ids, row_ids].add(tile_set * live_mask[:, None, None])
    placed = placed * scale_set[:, None, None, :]
    return placed.reshape(block_count, RB * TB, TB)


def place_panels(blocked, tile_set, row_ids, col_ids, live_mask, panel_count):
    picked = jnp.take(blocked, col_ids, axis=0)
    product = jnp.einsum("kac,kbc->kab", picked, tile_set, precision=lax.Precision.HIGHEST)
    product = product.reshape(panel_count, -1, RB * TB, TB)
    hit_row = (row_ids[:, None] == jnp.arange(RB, dtype=jnp.int32)[None, :]).astype(
        jnp.float32
    ) * live_mask[:, None]
    hit_row = hit_row.reshape(panel_count, -1, RB)
    placed = jnp.einsum("pkr,pkab->aprb", hit_row, product, precision=lax.Precision.HIGHEST)
    return placed.reshape(RB * TB, panel_count * RB * TB)


def per_device_any(tiles, tile_rows, tile_cols, counts, scaling):
    slot_total = tiles.shape[1]
    slot_range = jnp.arange(slot_total, dtype=jnp.int32)
    own_live = (slot_range < counts[0, 0]).astype(jnp.float32)
    blocked = densify(
        tiles[0], tile_rows[0], tile_cols[0], own_live, scaling.reshape(CB_DEV, TB), CB_DEV
    )
    piece_tiles = lax.all_gather(tiles, "rows", axis=0, tiled=True)
    piece_rows = lax.all_gather(tile_rows, "rows", axis=0, tiled=True)
    piece_cols = lax.all_gather(tile_cols, "rows", axis=0, tiled=True)
    piece_counts = lax.all_gather(counts, "rows", axis=0, tiled=True)
    count_here = piece_tiles.shape[0]
    live_mask = (slot_range[None, :] < piece_counts).astype(jnp.float32).reshape(-1)
    tile_block = place_panels(
        blocked,
        piece_tiles.reshape(count_here * slot_total, TB, TB),
        piece_rows.reshape(-1),
        piece_cols.reshape(-1),
        live_mask,
        count_here,
    )
    return lax.psum_scatter(tile_block, "cols", scatter_dimension=1, tiled=True)


def solution(mesh):
    placed = (
        P("rows", "cols", None, None),
        P("rows", "cols"),
        P("rows", "cols"),
        P("rows", "cols"),
        P("cols"),
    )
    small = mesh.shape["rows"] == 8 and mesh.shape["cols"] == 4
    return jax.shard_map(
        per_device if small else per_device_any,
        mesh=mesh,
        in_specs=placed,
        out_specs=P("rows", "cols"),
        check_vma=False,
    )
```

```python
import functools

import jax
import jax.numpy as jnp
from jax import lax
from jax.experimental import pallas as pl
from jax.experimental.pallas import tpu as pltpu
from jax.sharding import PartitionSpec as P

TB = 128
RB = 2
CB_DEV = 16
PANEL = RB * TB
META = 8
CUTS = 2
CUT = TB // CUTS
AXES = ("rows", "cols")
VMEM_LIMIT = 16 * 1024 * 1024
PACK_LIMIT = 60 * 1024 * 1024
VSPEC = pl.BlockSpec(memory_space=pltpu.VMEM)
HSPEC = pl.BlockSpec(memory_space=pltpu.HBM)


def params(limit=VMEM_LIMIT):
    return pltpu.CompilerParams(vmem_limit_bytes=limit)


def cost(flops, nbytes):
    return pl.CostEstimate(flops=flops * 20, bytes_accessed=nbytes * 20, transcendentals=0)


def pack_kernel(slots, rows_hbm, cols_hbm, counts_hbm, tiles_hbm, scale_hbm, *refs):
    whole_ref = refs[0]
    cut_refs = refs[1 : 1 + CUTS]
    rows_ref, cols_ref, counts_ref, tiles_ref, scale_ref, sems = refs[1 + CUTS :]
    copies = [
        pltpu.make_async_copy(source, target, sems.at[index])
        for index, (source, target) in enumerate(
            (
                (rows_hbm, rows_ref),
                (cols_hbm, cols_ref),
                (counts_hbm, counts_ref),
                (scale_hbm, scale_ref),
                (tiles_hbm, tiles_ref),
            )
        )
    ]
    for copy in copies:
        copy.start()
    for copy in copies[:4]:
        copy.wait()
    lane = lax.broadcasted_iota(jnp.int32, (META, TB), 1)
    codes = jnp.full((META, TB), -1.0, jnp.float32)
    count = counts_ref[0, 0]
    factors = []
    for slot in range(slots):
        live = slot < count
        row = rows_ref[0, slot]
        col = cols_ref[0, slot]
        factors.append(jnp.where(live, jnp.sqrt(scale_ref[pl.ds(col, 1), :]), 0.0))
        code = jnp.where(live, col * RB + row, -1).astype(jnp.float32)
        codes = jnp.where(lane == slot, code, codes)
    copies[4].wait()
    for slot in range(slots):
        for cut in range(CUTS):
            scaled = tiles_ref[0, slot, cut * CUT : (cut + 1) * CUT, :] * factors[slot]
            start = slot * CUT
            cut_refs[cut][start : start + CUT, :] = scaled
            start += cut * (slots * CUT + META)
            whole_ref[start : start + CUT, :] = scaled
    for cut in range(CUTS):
        cut_refs[cut][slots * CUT :, :] = codes
        start = cut * (slots * CUT + META) + slots * CUT
        whole_ref[start : start + META, :] = codes


def pack(tiles, tile_rows, tile_cols, counts, scaling):
    slots = tiles.shape[1]
    piece = slots * CUT + META
    return pl.pallas_call(
        functools.partial(pack_kernel, slots),
        out_shape=[jax.ShapeDtypeStruct((CUTS * piece, TB), jnp.float32)]
        + [jax.ShapeDtypeStruct((piece, TB), jnp.float32)] * CUTS,
        in_specs=[HSPEC] * 5,
        out_specs=[VSPEC] * (1 + CUTS),
        scratch_shapes=[
            pltpu.SMEM(tile_rows.shape, jnp.int32),
            pltpu.SMEM(tile_cols.shape, jnp.int32),
            pltpu.SMEM(counts.shape, jnp.int32),
            pltpu.VMEM(tiles.shape, jnp.float32),
            pltpu.VMEM((CB_DEV, TB), jnp.float32),
            pltpu.SemaphoreType.DMA((5,)),
        ],
        compiler_params=params(PACK_LIMIT),
        cost_estimate=cost(slots * TB * TB, 3 * slots * TB * TB * 4),
        name="pack",
    )(tile_rows, tile_cols, counts, tiles, scaling.reshape(CB_DEV, TB))


def read_codes(piece_refs, base, stage_ref, code_ref, sem):
    for index, piece_ref in enumerate(piece_refs):
        stage_ref[index] = piece_ref[base : base + META, :].astype(jnp.int32)
    copy = pltpu.make_async_copy(stage_ref, code_ref, sem)
    copy.start()
    copy.wait()


def code_scratch(count):
    return [
        pltpu.VMEM((count, META, TB), jnp.int32),
        pltpu.SMEM((count, META, TB), jnp.int32),
        pltpu.SMEM((CB_DEV,), jnp.int32),
        pltpu.SemaphoreType.DMA,
    ]


def mark(slots, code_ref, first_index, used_ref):
    for col in range(CB_DEV):
        used_ref[col] = 0
    for side in range(2):
        for slot in range(slots):
            code = code_ref[first_index + side, 0, slot]

            @pl.when(code >= 0)
            def _(code=code):
                used_ref[code >> 1] = 1


def spread_kernel(slots, count, *refs):
    pieces = refs[: 2 * count]
    dense_ref, sum_ref, stage_ref, code_ref, used_ref, sem = refs[2 * count :]
    cuts_each = CUTS // count
    read_codes((pieces[0], pieces[count]), slots * CUT, stage_ref, code_ref, sem)
    for col in range(CB_DEV):
        used_ref[col] = 0
    for side in range(2):
        for slot in range(slots):
            code = code_ref[side, 0, slot]

            @pl.when(code >= 0)
            def _(code=code, slot=slot, side=side):
                col = code >> 1

                @pl.when(used_ref[col] == 0)
                def _():
                    used_ref[col] = 1
                    sum_ref[col] = jnp.zeros_like(sum_ref[col])

                start = pl.multiple_of(side * PANEL + (code & 1) * TB, TB)
                for cut in range(CUTS):
                    piece_ref = pieces[side * count + cut // cuts_each]
                    base = (cut % cuts_each) * (slots * CUT + META) + slot * CUT
                    place = pl.ds(start + cut * CUT, CUT)
                    sum_ref[col, place, :] += piece_ref[base : base + CUT, :]

    def convert(col, carry):
        @pl.when(used_ref[col] == 1)
        def _():
            high, low = split(sum_ref[col])
            dense_ref[col, :, :TB] = high
            dense_ref[col, :, TB:] = low

        return carry

    lax.fori_loop(0, CB_DEV, convert, 0)


def spread(own, other, slots):
    count = len(own)
    return pl.pallas_call(
        functools.partial(spread_kernel, slots, count),
        out_shape=jax.ShapeDtypeStruct((CB_DEV, 2 * PANEL, 2 * TB), jnp.bfloat16),
        in_specs=[VSPEC] * (2 * count),
        out_specs=VSPEC,
        scratch_shapes=[
            pltpu.VMEM((CB_DEV, 2 * PANEL, TB), jnp.float32),
            *code_scratch(2),
        ],
        compiler_params=params(),
        cost_estimate=cost(1 << 20, 1 << 21),
        name="spread",
    )(*own, *other)


def split(x):
    high = x.astype(jnp.bfloat16)
    low = (x - high.astype(jnp.float32)).astype(jnp.bfloat16)
    return high, low


def nt_dot(a, b):
    return lax.dot_general(a, b, (((1,), (1,)), ((), ())), preferred_element_type=jnp.float32)


def product(left, tile):
    high, low = split(tile)
    right = jnp.concatenate(
        [jnp.concatenate([high, high], axis=1), jnp.concatenate([low, low], axis=1)], axis=0
    )
    return nt_dot(left, right)


def swapped():
    chip = lax.axis_index("rows") >> 1
    plane = lax.axis_index("cols")
    chip_outer = (chip == 0) | (chip == 3)
    plane_outer = (plane == 0) | (plane == 3)
    chunk_a = jnp.where(plane_outer, chip, chip ^ 1)
    near = jnp.where(chip_outer, plane, plane ^ 1)
    return jnp.where(chunk_a == near, 0, 1).astype(jnp.int32)


def for_live(slots, code_ref, used_ref, flag, body):
    for which in range(2):
        chunk = flag if which == 0 else 1 - flag
        for slot in range(slots):
            code = code_ref[which, 0, slot]
            live = (code >= 0) & (used_ref[jnp.maximum(code, 0) >> 1] == 1)

            @pl.when(live)
            def _(code=code, which=which, slot=slot, chunk=chunk):
                body(which, slot, code >> 1, chunk, code & 1)


def first_kernel(slots, dense_ref, own_ref, other_ref, a_ref, b_ref, acc_ref, stage_ref, code_ref, used_ref, sem):
    read_codes((a_ref, b_ref, own_ref, other_ref), slots * CUT, stage_ref, code_ref, sem)
    mark(slots, code_ref, 2, used_ref)
    acc_ref[...] = jnp.zeros_like(acc_ref)

    def body(which, slot, col, chunk, block):
        piece_ref = a_ref if which == 0 else b_ref
        starts = [cut * (slots * CUT + META) + slot * CUT for cut in range(CUTS)]
        tile = jnp.concatenate([piece_ref[start : start + CUT, :] for start in starts], axis=0)
        both = product(dense_ref[col], tile)
        acc_ref[chunk, block] += both[:, :TB] + both[:, TB:]

    for_live(slots, code_ref, used_ref, swapped(), body)


def first(dense, own, other, right_a, right_b, slots):
    return pl.pallas_call(
        functools.partial(first_kernel, slots),
        out_shape=jax.ShapeDtypeStruct((2, RB, 2 * PANEL, TB), jnp.float32),
        in_specs=[VSPEC] * 5,
        out_specs=VSPEC,
        scratch_shapes=code_scratch(4),
        compiler_params=params(),
        cost_estimate=cost(slots * 4 * 4 * PANEL * TB * TB, 1 << 22),
        name="first",
    )(dense, own, other, right_a, right_b)


def second_kernel(slots, cut, dense_ref, own_ref, other_ref, acc_ref, a_ref, b_ref, *refs):
    out_refs = refs[:4]
    sum_ref, stage_ref, code_ref, used_ref, sem = refs[4:]
    read_codes((a_ref, b_ref, own_ref, other_ref), slots * CUT, stage_ref, code_ref, sem)
    mark(slots, code_ref, 2, used_ref)
    sum_ref[...] = jnp.zeros_like(sum_ref)

    def body(which, slot, col, chunk, block):
        piece_ref = a_ref if which == 0 else b_ref
        sum_ref[chunk, block] += product(dense_ref[col], piece_ref[slot * CUT : (slot + 1) * CUT, :])

    for_live(slots, code_ref, used_ref, swapped(), body)
    for chunk in range(2):
        for side in range(2):
            rows = slice(side * PANEL, (side + 1) * PANEL)
            parts = []
            for block in range(RB):
                both = sum_ref[chunk, block, rows, :]
                parts.append(both[:, :CUT] + both[:, CUT:] + acc_ref[chunk, block, rows, cut * CUT : (cut + 1) * CUT])
            out_refs[2 * chunk + side][...] = jnp.concatenate(parts, axis=1)


def second(cut, dense, own, other, acc, piece_a, piece_b, slots):
    shape = jax.ShapeDtypeStruct((PANEL, RB * CUT), jnp.float32)
    return pl.pallas_call(
        functools.partial(second_kernel, slots, cut),
        out_shape=[shape] * 4,
        in_specs=[VSPEC] * 6,
        out_specs=[VSPEC] * 4,
        scratch_shapes=[
            pltpu.VMEM((2, RB, 2 * PANEL, 2 * CUT), jnp.float32),
            *code_scratch(4),
        ],
        compiler_params=params(),
        cost_estimate=cost(slots * 2 * 4 * PANEL * TB * TB, 1 << 21),
        name="second",
    )(dense, own, other, acc, piece_a, piece_b)


def join_kernel(cuts, cut_rows, *refs):
    out_ref = refs[-1]
    core = lax.axis_index("rows") & 1
    for side in range(2):
        halves = [refs[side * cuts + cut][...] + refs[(2 + side) * cuts + cut][...] for cut in range(cuts)]
        for block in range(RB):
            part = [half[:, block * cut_rows : (block + 1) * cut_rows] for half in halves]
            panel = core if side == 0 else 1 - core
            start = pl.multiple_of(panel * PANEL + block * TB, TB)
            out_ref[:, pl.ds(start, TB)] = part[0] if cuts == 1 else jnp.concatenate(part, axis=1)


def join(near_same, near_cross, far_same, far_cross):
    cuts = len(near_same)
    return pl.pallas_call(
        functools.partial(join_kernel, cuts, TB // cuts),
        out_shape=jax.ShapeDtypeStruct((PANEL, 2 * PANEL), jnp.float32),
        in_specs=[VSPEC] * (4 * cuts),
        out_specs=VSPEC,
        compiler_params=params(),
        cost_estimate=cost(PANEL * 2 * PANEL, PANEL * 2 * PANEL * 12),
        name="join",
    )(*near_same, *near_cross, *far_same, *far_cross)


def pairs(place):
    out = []
    for row in range(8):
        for col in range(4):
            chip, core, plane = place(row >> 1, row & 1, col)
            out.append((row * 4 + col, (chip * 2 + core) * 4 + plane))
    return out


def outer(plane):
    return plane in (0, 3)


SWAP = pairs(lambda k, i, p: (k, 1 - i, p))
NEXT = pairs(lambda k, i, p: (k, i, p ^ 1))
SEND_A = pairs(lambda k, i, p: (k if outer(p) else k ^ 1, i, p))
SEND_B = pairs(lambda k, i, p: (k ^ 3 if outer(p) else k ^ 2, i, p))
NEAR = pairs(lambda k, i, p: (k, i, p if outer(k) else p ^ 1))
FAR = pairs(lambda k, i, p: (k, i, p ^ 3 if outer(k) else p ^ 2))
NEAR_CROSS = pairs(lambda k, i, p: (k, 1 - i, p if outer(k) else p ^ 1))
FAR_CROSS = pairs(lambda k, i, p: (k, 1 - i, p ^ 3 if outer(k) else p ^ 2))


def send(pieces, perm):
    return [lax.ppermute(piece, AXES, perm) for piece in pieces]


def after(x, *others):
    return lax.optimization_barrier((x, *others))[0]


def per_device(tiles, tile_rows, tile_cols, counts, scaling):
    slots = tiles.shape[1]
    whole, *own = pack(tiles, tile_rows, tile_cols, counts, scaling)
    next_own = send(own, NEXT)
    own_a, own_b = (lax.ppermute(whole, AXES, perm) for perm in (SEND_A, SEND_B))
    own_other = lax.ppermute(whole, AXES, SWAP)
    own_dense = spread([whole], [own_other], slots)
    acc = first(own_dense, whole, own_other, own_a, own_b, slots)
    early = after(next_own[1], own_dense)
    late = after(next_own[0], acc)
    next_a = send((late, early), SEND_A)
    next_b = send((late, early), SEND_B)
    next_other = send((after(next_own[0], own_b), after(next_own[1], own_a)), SWAP)
    next_dense = spread(next_own, next_other, slots)
    near_same, near_cross, far_same, far_cross = [], [], [], []
    for cut in range(CUTS):
        results = second(cut, next_dense, next_own[0], next_other[0], acc, next_a[cut], next_b[cut], slots)
        far_same.append(lax.ppermute(results[2], AXES, FAR))
        far_cross.append(lax.ppermute(results[3], AXES, FAR_CROSS))
        near_same.append(lax.ppermute(results[0], AXES, NEAR))
        near_cross.append(lax.ppermute(results[1], AXES, NEAR_CROSS))
    return join(near_same, near_cross, far_same, far_cross)


def densify(tile_set, row_ids, col_ids, live_mask, scale_set, block_count):
    placed = jnp.zeros((block_count, RB, TB, TB), jnp.float32)
    placed = placed.at[col_ids, row_ids].add(tile_set * live_mask[:, None, None])
    placed = placed * scale_set[:, None, None, :]
    return placed.reshape(block_count, RB * TB, TB)


def place_panels(blocked, tile_set, row_ids, col_ids, live_mask, panel_count):
    picked = jnp.take(blocked, col_ids, axis=0)
    product = jnp.einsum("kac,kbc->kab", picked, tile_set, precision=lax.Precision.HIGHEST)
    product = product.reshape(panel_count, -1, RB * TB, TB)
    hit_row = (row_ids[:, None] == jnp.arange(RB, dtype=jnp.int32)[None, :]).astype(
        jnp.float32
    ) * live_mask[:, None]
    hit_row = hit_row.reshape(panel_count, -1, RB)
    placed = jnp.einsum("pkr,pkab->aprb", hit_row, product, precision=lax.Precision.HIGHEST)
    return placed.reshape(RB * TB, panel_count * RB * TB)


def per_device_any(tiles, tile_rows, tile_cols, counts, scaling):
    slot_total = tiles.shape[1]
    slot_range = jnp.arange(slot_total, dtype=jnp.int32)
    own_live = (slot_range < counts[0, 0]).astype(jnp.float32)
    blocked = densify(
        tiles[0], tile_rows[0], tile_cols[0], own_live, scaling.reshape(CB_DEV, TB), CB_DEV
    )
    piece_tiles = lax.all_gather(tiles, "rows", axis=0, tiled=True)
    piece_rows = lax.all_gather(tile_rows, "rows", axis=0, tiled=True)
    piece_cols = lax.all_gather(tile_cols, "rows", axis=0, tiled=True)
    piece_counts = lax.all_gather(counts, "rows", axis=0, tiled=True)
    count_here = piece_tiles.shape[0]
    live_mask = (slot_range[None, :] < piece_counts).astype(jnp.float32).reshape(-1)
    tile_block = place_panels(
        blocked,
        piece_tiles.reshape(count_here * slot_total, TB, TB),
        piece_rows.reshape(-1),
        piece_cols.reshape(-1),
        live_mask,
        count_here,
    )
    return lax.psum_scatter(tile_block, "cols", scatter_dimension=1, tiled=True)


def solution(mesh):
    placed = (
        P("rows", "cols", None, None),
        P("rows", "cols"),
        P("rows", "cols"),
        P("rows", "cols"),
        P("cols"),
    )
    small = mesh.shape["rows"] == 8 and mesh.shape["cols"] == 4
    return jax.shard_map(
        per_device if small else per_device_any,
        mesh=mesh,
        in_specs=placed,
        out_specs=P("rows", "cols"),
        check_vma=False,
    )
```

```python
import functools

import jax
import jax.numpy as jnp
from jax import lax
from jax.experimental import pallas as pl
from jax.experimental.pallas import tpu as pltpu
from jax.sharding import PartitionSpec as P

TB = 128
RB = 2
CB_DEV = 16
PANEL = RB * TB
META = 8
FEW = 5
CUTS = 2
CUT = TB // CUTS
AXES = ("rows", "cols")
VMEM_LIMIT = 16 * 1024 * 1024
PACK_LIMIT = 60 * 1024 * 1024
VSPEC = pl.BlockSpec(memory_space=pltpu.VMEM)
HSPEC = pl.BlockSpec(memory_space=pltpu.HBM)


def params(limit=VMEM_LIMIT):
    return pltpu.CompilerParams(vmem_limit_bytes=limit)


def cost(flops, nbytes):
    return pl.CostEstimate(flops=flops * 20, bytes_accessed=nbytes * 20, transcendentals=0)


def pack_kernel(slots, rows_hbm, cols_hbm, counts_hbm, tiles_hbm, scale_hbm, *refs):
    whole_ref, rows_ref, cols_ref, counts_ref, tiles_ref, scale_ref, sems = refs
    copies = [
        pltpu.make_async_copy(source, target, sems.at[index])
        for index, (source, target) in enumerate(
            (
                (rows_hbm, rows_ref),
                (cols_hbm, cols_ref),
                (counts_hbm, counts_ref),
                (scale_hbm, scale_ref),
                (tiles_hbm, tiles_ref),
            )
        )
    ]
    for copy in copies:
        copy.start()
    for copy in copies[:4]:
        copy.wait()
    lane = lax.broadcasted_iota(jnp.int32, (META, TB), 1)
    codes = jnp.full((META, TB), -1.0, jnp.float32)
    count = counts_ref[0, 0]
    factors = []
    for slot in range(slots):
        live = slot < count
        row = rows_ref[0, slot]
        col = cols_ref[0, slot]
        factors.append(jnp.where(live, jnp.sqrt(scale_ref[pl.ds(col, 1), :]), 0.0))
        code = jnp.where(live, col * RB + row, -1).astype(jnp.float32)
        codes = jnp.where(lane == slot, code, codes)
    copies[4].wait()
    for slot in range(slots):
        for cut in range(CUTS):
            start = cut * (slots * CUT + META) + slot * CUT
            part = tiles_ref[0, slot, cut * CUT : (cut + 1) * CUT, :]
            whole_ref[start : start + CUT, :] = part * factors[slot]
    for cut in range(CUTS):
        start = cut * (slots * CUT + META) + slots * CUT
        whole_ref[start : start + META, :] = codes


def pack(tiles, tile_rows, tile_cols, counts, scaling):
    slots = tiles.shape[1]
    piece = slots * CUT + META
    return pl.pallas_call(
        functools.partial(pack_kernel, slots),
        out_shape=jax.ShapeDtypeStruct((CUTS * piece, TB), jnp.float32),
        in_specs=[HSPEC] * 5,
        out_specs=VSPEC,
        scratch_shapes=[
            pltpu.SMEM(tile_rows.shape, jnp.int32),
            pltpu.SMEM(tile_cols.shape, jnp.int32),
            pltpu.SMEM(counts.shape, jnp.int32),
            pltpu.VMEM(tiles.shape, jnp.float32),
            pltpu.VMEM((CB_DEV, TB), jnp.float32),
            pltpu.SemaphoreType.DMA((5,)),
        ],
        compiler_params=params(PACK_LIMIT),
        cost_estimate=cost(slots * TB * TB, 3 * slots * TB * TB * 4),
        name="pack",
    )(tile_rows, tile_cols, counts, tiles, scaling.reshape(CB_DEV, TB))


def read_codes(piece_ref, slots):
    row = piece_ref[slots * CUT : slots * CUT + META, :].astype(jnp.int32)
    return [row[0, slot] for slot in range(slots)]


def spread_kernel(slots, own_ref, other_ref, dense_ref, sum_ref, used_ref):
    codes = [read_codes(piece_ref, slots) for piece_ref in (own_ref, other_ref)]
    for col in range(CB_DEV):
        used_ref[col] = 0
    for side in range(2):
        for slot in range(slots):
            code = codes[side][slot]

            @pl.when(code >= 0)
            def _(code=code, slot=slot, side=side):
                col = code >> 1

                @pl.when(used_ref[col] == 0)
                def _():
                    used_ref[col] = 1
                    sum_ref[col] = jnp.zeros_like(sum_ref[col])

                start = pl.multiple_of(side * PANEL + (code & 1) * TB, TB)
                for cut in range(CUTS):
                    piece_ref = own_ref if side == 0 else other_ref
                    base = cut * (slots * CUT + META) + slot * CUT
                    place = pl.ds(start + cut * CUT, CUT)
                    sum_ref[col, place, :] += piece_ref[base : base + CUT, :]

    def convert(col, carry):
        @pl.when(used_ref[col] == 1)
        def _():
            high, low = split(sum_ref[col])
            dense_ref[col, :, :TB] = high
            dense_ref[col, :, TB:] = low

        @pl.when(used_ref[col] == 0)
        def _():
            dense_ref[col] = jnp.zeros_like(dense_ref[col])

        return carry

    lax.fori_loop(0, CB_DEV, convert, 0)


def spread(own, other, slots):
    return pl.pallas_call(
        functools.partial(spread_kernel, slots),
        out_shape=jax.ShapeDtypeStruct((CB_DEV, 2 * PANEL, 2 * TB), jnp.bfloat16),
        in_specs=[VSPEC] * 2,
        out_specs=VSPEC,
        scratch_shapes=[
            pltpu.VMEM((CB_DEV, 2 * PANEL, TB), jnp.float32),
            pltpu.SMEM((CB_DEV,), jnp.int32),
        ],
        compiler_params=params(),
        cost_estimate=cost(1 << 20, 1 << 21),
        name="spread",
    )(own, other)


def split(x):
    high = x.astype(jnp.bfloat16)
    low = (x - high.astype(jnp.float32)).astype(jnp.bfloat16)
    return high, low


def nt_dot(a, b):
    return lax.dot_general(a, b, (((1,), (1,)), ((), ())), preferred_element_type=jnp.float32)


def product(left, tile):
    high, low = split(tile)
    right = jnp.concatenate(
        [jnp.concatenate([high, high], axis=1), jnp.concatenate([low, low], axis=1)], axis=0
    )
    return nt_dot(left, right)


def for_tiles(slots, piece_refs, body):
    codes = [read_codes(piece_ref, slots) for piece_ref in piece_refs]
    core = lax.axis_index("rows") & 1

    def some(which, slot_range):
        for slot in slot_range:
            code = jnp.maximum(codes[which][slot], 0)
            body(which, slot, code >> 1, core if which == 0 else 1 - core, code & 1)

    few = min(FEW, slots)
    for which in range(2):
        some(which, range(few))
    if few < slots:
        for which in range(2):

            @pl.when(codes[which][few] >= 0)
            def _(which=which):
                some(which, range(few, slots))


def first_kernel(slots, dense_ref, a_ref, b_ref, acc_ref):
    acc_ref[...] = jnp.zeros_like(acc_ref)

    def body(which, slot, col, panel, block):
        piece_ref = a_ref if which == 0 else b_ref
        starts = [cut * (slots * CUT + META) + slot * CUT for cut in range(CUTS)]
        tile = jnp.concatenate([piece_ref[start : start + CUT, :] for start in starts], axis=0)
        both = product(dense_ref[col], tile)
        acc_ref[panel, block] += both[:, :TB] + both[:, TB:]

    for_tiles(slots, (a_ref, b_ref), body)


def first(dense, right_a, right_b, slots):
    return pl.pallas_call(
        functools.partial(first_kernel, slots),
        out_shape=jax.ShapeDtypeStruct((2, RB, 2 * PANEL, TB), jnp.float32),
        in_specs=[VSPEC] * 3,
        out_specs=VSPEC,
        compiler_params=params(),
        cost_estimate=cost(slots * 4 * 4 * PANEL * TB * TB, 1 << 22),
        name="first",
    )(dense, right_a, right_b)


def second_kernel(slots, cut, dense_ref, acc_ref, a_ref, b_ref, own_ref, other_ref, sum_ref):
    sum_ref[...] = jnp.zeros_like(sum_ref)

    def body(which, slot, col, panel, block):
        piece_ref = a_ref if which == 0 else b_ref
        sum_ref[panel, block] += product(dense_ref[col], piece_ref[slot * CUT : (slot + 1) * CUT, :])

    for_tiles(slots, (a_ref, b_ref), body)
    for side, out_ref in enumerate((own_ref, other_ref)):
        rows = slice(side * PANEL, (side + 1) * PANEL)
        parts = []
        for panel in range(2):
            for block in range(RB):
                both = sum_ref[panel, block, rows, :]
                before = acc_ref[panel, block, rows, cut * CUT : (cut + 1) * CUT]
                parts.append(both[:, :CUT] + both[:, CUT:] + before)
        out_ref[...] = jnp.concatenate(parts, axis=1)


def second(cut, dense, acc, piece_a, piece_b, slots):
    shape = jax.ShapeDtypeStruct((PANEL, 2 * RB * CUT), jnp.float32)
    return pl.pallas_call(
        functools.partial(second_kernel, slots, cut),
        out_shape=[shape] * 2,
        in_specs=[VSPEC] * 4,
        out_specs=[VSPEC] * 2,
        scratch_shapes=[pltpu.VMEM((2, RB, 2 * PANEL, 2 * CUT), jnp.float32)],
        compiler_params=params(),
        cost_estimate=cost(slots * 2 * 4 * PANEL * TB * TB, 1 << 21),
        name="second",
    )(dense, acc, piece_a, piece_b)


def join_kernel(*refs):
    out_ref = refs[-1]
    for place in range(2 * RB):
        lanes = slice(place * CUT, (place + 1) * CUT)
        parts = [refs[cut][:, lanes] + refs[CUTS + cut][:, lanes] for cut in range(CUTS)]
        out_ref[:, place * TB : (place + 1) * TB] = parts[0] if CUTS == 1 else jnp.concatenate(parts, axis=1)


def join(from_same, from_cross):
    return pl.pallas_call(
        join_kernel,
        out_shape=jax.ShapeDtypeStruct((PANEL, 2 * PANEL), jnp.float32),
        in_specs=[VSPEC] * (2 * CUTS),
        out_specs=VSPEC,
        compiler_params=params(),
        cost_estimate=cost(1 << 17, 1 << 17),
        name="join",
    )(*from_same, *from_cross)


def chunk(k, i, p):
    return k ^ p ^ (3 * i)


def pairs(place):
    out = []
    for row in range(8):
        for col in range(4):
            chip, core, plane = place(row >> 1, row & 1, col)
            out.append((row * 4 + col, (chip * 2 + core) * 4 + plane))
    return out


SWAP = pairs(lambda k, i, p: (k, 1 - i, p))
NEXT = pairs(lambda k, i, p: (k, i, p ^ 1))
SEND_SAME = pairs(lambda k, i, p: (chunk(k, i, p), i, p))
SEND_CROSS = pairs(lambda k, i, p: (chunk(k, 1 - i, p), 1 - i, p))
DONE_SAME = pairs(lambda k, i, p: (k, i, chunk(k, i, p)))
DONE_CROSS = pairs(lambda k, i, p: (k, 1 - i, chunk(k, i, p)))


def send(pieces, perms):
    return [lax.ppermute(piece, AXES, perm) for piece, perm in zip(pieces, perms)]


def after(x, *others):
    return lax.optimization_barrier((x, *others))[0]


def per_device(tiles, tile_rows, tile_cols, counts, scaling):
    slots = tiles.shape[1]
    own = pack(tiles, tile_rows, tile_cols, counts, scaling)
    piece = slots * CUT + META
    near_own = lax.ppermute(own, AXES, NEXT)
    own_a, own_b, own_other = send([own] * 3, (SEND_SAME, SEND_CROSS, SWAP))
    own_dense = spread(own, own_other, slots)
    acc = first(own_dense, own_a, own_b, slots)
    near_other = lax.ppermute(after(near_own, own_dense), AXES, SWAP)
    near_dense = spread(near_own, near_other, slots)
    starts = (after(near_own, own_dense), after(near_own, own_dense))
    from_same, from_cross = [], []
    for cut in range(CUTS):
        part = lax.slice_in_dim(starts[cut], cut * piece, (cut + 1) * piece)
        part_a, part_b = send([part] * 2, (SEND_SAME, SEND_CROSS))
        kept, other = second(cut, near_dense, acc, part_a, part_b, slots)
        from_same.append(lax.ppermute(kept, AXES, DONE_SAME))
        from_cross.append(lax.ppermute(other, AXES, DONE_CROSS))
    return join(from_same, from_cross)


def densify(tile_set, row_ids, col_ids, live_mask, scale_set, block_count):
    placed = jnp.zeros((block_count, RB, TB, TB), jnp.float32)
    placed = placed.at[col_ids, row_ids].add(tile_set * live_mask[:, None, None])
    placed = placed * scale_set[:, None, None, :]
    return placed.reshape(block_count, RB * TB, TB)


def place_panels(blocked, tile_set, row_ids, col_ids, live_mask, panel_count):
    picked = jnp.take(blocked, col_ids, axis=0)
    product = jnp.einsum("kac,kbc->kab", picked, tile_set, precision=lax.Precision.HIGHEST)
    product = product.reshape(panel_count, -1, RB * TB, TB)
    hit_row = (row_ids[:, None] == jnp.arange(RB, dtype=jnp.int32)[None, :]).astype(
        jnp.float32
    ) * live_mask[:, None]
    hit_row = hit_row.reshape(panel_count, -1, RB)
    placed = jnp.einsum("pkr,pkab->aprb", hit_row, product, precision=lax.Precision.HIGHEST)
    return placed.reshape(RB * TB, panel_count * RB * TB)


def per_device_any(tiles, tile_rows, tile_cols, counts, scaling):
    slot_total = tiles.shape[1]
    slot_range = jnp.arange(slot_total, dtype=jnp.int32)
    own_live = (slot_range < counts[0, 0]).astype(jnp.float32)
    blocked = densify(
        tiles[0], tile_rows[0], tile_cols[0], own_live, scaling.reshape(CB_DEV, TB), CB_DEV
    )
    piece_tiles = lax.all_gather(tiles, "rows", axis=0, tiled=True)
    piece_rows = lax.all_gather(tile_rows, "rows", axis=0, tiled=True)
    piece_cols = lax.all_gather(tile_cols, "rows", axis=0, tiled=True)
    piece_counts = lax.all_gather(counts, "rows", axis=0, tiled=True)
    count_here = piece_tiles.shape[0]
    live_mask = (slot_range[None, :] < piece_counts).astype(jnp.float32).reshape(-1)
    tile_block = place_panels(
        blocked,
        piece_tiles.reshape(count_here * slot_total, TB, TB),
        piece_rows.reshape(-1),
        piece_cols.reshape(-1),
        live_mask,
        count_here,
    )
    return lax.psum_scatter(tile_block, "cols", scatter_dimension=1, tiled=True)


def solution(mesh):
    placed = (
        P("rows", "cols", None, None),
        P("rows", "cols"),
        P("rows", "cols"),
        P("rows", "cols"),
        P("cols"),
    )
    small = mesh.shape["rows"] == 8 and mesh.shape["cols"] == 4
    return jax.shard_map(
        per_device if small else per_device_any,
        mesh=mesh,
        in_specs=placed,
        out_specs=P("rows", "cols"),
        check_vma=False,
    )
```

```python
import functools

import jax
import jax.numpy as jnp
from jax import lax
from jax.experimental import pallas as pl
from jax.experimental.pallas import tpu as pltpu
from jax.sharding import PartitionSpec as P

TB = 128
RB = 2
CB_DEV = 16
PANEL = RB * TB
META = 8
FEW = 5
AXES = ("rows", "cols")
VMEM_LIMIT = 16 * 1024 * 1024
PACK_LIMIT = 60 * 1024 * 1024
VSPEC = pl.BlockSpec(memory_space=pltpu.VMEM)
HSPEC = pl.BlockSpec(memory_space=pltpu.HBM)


def params(limit=VMEM_LIMIT):
    return pltpu.CompilerParams(vmem_limit_bytes=limit)


def cost(flops, nbytes):
    return pl.CostEstimate(flops=flops, bytes_accessed=nbytes, transcendentals=0)


def pack_kernel(slots, rows_hbm, cols_hbm, counts_hbm, tiles_hbm, scale_hbm, *refs):
    whole_ref, rows_ref, cols_ref, counts_ref, tiles_ref, scale_ref, sems = refs
    copies = [
        pltpu.make_async_copy(source, target, sems.at[index])
        for index, (source, target) in enumerate(
            (
                (rows_hbm, rows_ref),
                (cols_hbm, cols_ref),
                (counts_hbm, counts_ref),
                (scale_hbm, scale_ref),
                (tiles_hbm, tiles_ref),
            )
        )
    ]
    for copy in copies:
        copy.start()
    for copy in copies[:4]:
        copy.wait()
    lane = lax.broadcasted_iota(jnp.int32, (META, TB), 1)
    codes = jnp.full((META, TB), -1.0, jnp.float32)
    count = counts_ref[0, 0]
    factors = []
    for slot in range(slots):
        live = slot < count
        row = rows_ref[0, slot]
        col = cols_ref[0, slot]
        factors.append(jnp.where(live, jnp.sqrt(scale_ref[pl.ds(col, 1), :]), 0.0))
        code = jnp.where(live, col * RB + row, -1).astype(jnp.float32)
        codes = jnp.where(lane == slot, code, codes)
    copies[4].wait()
    for slot in range(slots):
        whole_ref[slot * TB : (slot + 1) * TB, :] = tiles_ref[0, slot] * factors[slot]
    whole_ref[slots * TB :, :] = codes


def pack(tiles, tile_rows, tile_cols, counts, scaling):
    slots = tiles.shape[1]
    return pl.pallas_call(
        functools.partial(pack_kernel, slots),
        out_shape=jax.ShapeDtypeStruct((slots * TB + META, TB), jnp.float32),
        in_specs=[HSPEC] * 5,
        out_specs=VSPEC,
        scratch_shapes=[
            pltpu.SMEM(tile_rows.shape, jnp.int32),
            pltpu.SMEM(tile_cols.shape, jnp.int32),
            pltpu.SMEM(counts.shape, jnp.int32),
            pltpu.VMEM(tiles.shape, jnp.float32),
            pltpu.VMEM((CB_DEV, TB), jnp.float32),
            pltpu.SemaphoreType.DMA((5,)),
        ],
        compiler_params=params(PACK_LIMIT),
        cost_estimate=cost(slots * TB * TB, 3 * slots * TB * TB * 4),
        name="pack",
    )(tile_rows, tile_cols, counts, tiles, scaling.reshape(CB_DEV, TB))


def read_codes(piece_ref, slots):
    row = piece_ref[slots * TB : slots * TB + META, :].astype(jnp.int32)
    return [row[0, slot] for slot in range(slots)]


def spread_kernel(slots, own_ref, other_ref, dense_ref, sum_ref, used_ref):
    codes = [read_codes(piece_ref, slots) for piece_ref in (own_ref, other_ref)]
    for col in range(CB_DEV):
        used_ref[col] = 0
    for side in range(2):
        for slot in range(slots):
            code = codes[side][slot]

            @pl.when(code >= 0)
            def _(code=code, slot=slot, side=side):
                col = code >> 1

                @pl.when(used_ref[col] == 0)
                def _():
                    used_ref[col] = 1
                    sum_ref[col] = jnp.zeros_like(sum_ref[col])

                start = pl.multiple_of(side * PANEL + (code & 1) * TB, TB)
                piece_ref = own_ref if side == 0 else other_ref
                sum_ref[col, pl.ds(start, TB), :] += piece_ref[slot * TB : (slot + 1) * TB, :]

    def convert(col, carry):
        @pl.when(used_ref[col] == 1)
        def _():
            high, low = split(sum_ref[col])
            dense_ref[col, :, :TB] = high
            dense_ref[col, :, TB:] = low

        @pl.when(used_ref[col] == 0)
        def _():
            dense_ref[col] = jnp.zeros_like(dense_ref[col])

        return carry

    lax.fori_loop(0, CB_DEV, convert, 0)


def spread(own, other, slots):
    return pl.pallas_call(
        functools.partial(spread_kernel, slots),
        out_shape=jax.ShapeDtypeStruct((CB_DEV, 2 * PANEL, 2 * TB), jnp.bfloat16),
        in_specs=[VSPEC] * 2,
        out_specs=VSPEC,
        scratch_shapes=[
            pltpu.VMEM((CB_DEV, 2 * PANEL, TB), jnp.float32),
            pltpu.SMEM((CB_DEV,), jnp.int32),
        ],
        compiler_params=params(),
        cost_estimate=cost(1 << 25, 1 << 25),
        name="spread",
    )(own, other)


def split(x):
    high = x.astype(jnp.bfloat16)
    low = (x - high.astype(jnp.float32)).astype(jnp.bfloat16)
    return high, low


def nt_dot(a, b):
    return lax.dot_general(a, b, (((1,), (1,)), ((), ())), preferred_element_type=jnp.float32)


def product(left, tile):
    high, low = split(tile)
    right = jnp.concatenate(
        [jnp.concatenate([high, high], axis=1), jnp.concatenate([low, low], axis=1)], axis=0
    )
    return nt_dot(left, right)


def multiply_kernel(slots, *refs):
    dense_refs, piece_refs = refs[:2], refs[2:4]
    kept_ref, other_ref, sum_ref = refs[4:]
    sum_ref[...] = jnp.zeros_like(sum_ref)
    codes = [read_codes(piece_ref, slots) for piece_ref in piece_refs]

    def some(group, slot_range):
        for slot in slot_range:
            code = jnp.maximum(codes[group][slot], 0)
            tile = piece_refs[group][slot * TB : (slot + 1) * TB, :]
            both = product(dense_refs[group][code >> 1], tile)
            sum_ref[code & 1] += both[:, :TB] + both[:, TB:]

    few = min(FEW, slots)
    for group in range(2):
        some(group, range(few))
    if few < slots:
        for group in range(2):

            @pl.when(codes[group][few] >= 0)
            def _(group=group):
                some(group, range(few, slots))

    for block in range(RB):
        lanes = slice(block * TB, (block + 1) * TB)
        kept_ref[:, lanes] = sum_ref[block, :PANEL, :]
        other_ref[:, lanes] = sum_ref[block, PANEL:, :]


def multiply(denses, pieces, slots):
    return pl.pallas_call(
        functools.partial(multiply_kernel, slots),
        out_shape=[jax.ShapeDtypeStruct((PANEL, PANEL), jnp.float32)] * 2,
        in_specs=[VSPEC] * 4,
        out_specs=[VSPEC] * 2,
        scratch_shapes=[pltpu.VMEM((RB, 2 * PANEL, TB), jnp.float32)],
        compiler_params=params(),
        cost_estimate=cost(1 << 25, 1 << 25),
        name="multiply",
    )(*denses, *pieces)


def join_kernel(same_own_ref, same_far_ref, cross_own_ref, cross_far_ref, out_ref):
    core = lax.axis_index("rows") & 1
    start = pl.multiple_of(core * PANEL, PANEL)
    out_ref[:, pl.ds(start, PANEL)] = same_own_ref[...] + cross_far_ref[...]
    out_ref[:, pl.ds(PANEL - start, PANEL)] = same_far_ref[...] + cross_own_ref[...]


def join(*results):
    return pl.pallas_call(
        join_kernel,
        out_shape=jax.ShapeDtypeStruct((PANEL, 2 * PANEL), jnp.float32),
        in_specs=[VSPEC] * 4,
        out_specs=VSPEC,
        compiler_params=params(),
        cost_estimate=cost(1 << 17, 1 << 17),
        name="join",
    )(*results)


def chunk(k, i, p):
    return k ^ p ^ (3 * (i ^ (p & 1) ^ (p >> 1)))


def pairs(place):
    out = []
    for row in range(8):
        for col in range(4):
            chip, core, plane = place(row >> 1, row & 1, col)
            out.append((row * 4 + col, (chip * 2 + core) * 4 + plane))
    return out


SWAP = pairs(lambda k, i, p: (k, 1 - i, p))
NEXT = pairs(lambda k, i, p: (k, i, p ^ 1))
SEND_SAME = pairs(lambda k, i, p: (chunk(k, i, p), i, p))
SEND_CROSS = pairs(lambda k, i, p: (chunk(k, 1 - i, p), 1 - i, p))
DONE_SAME = pairs(lambda k, i, p: (k, i, chunk(k, i, p)))
DONE_CROSS = pairs(lambda k, i, p: (k, 1 - i, chunk(k, i, p)))


def send(pieces, perms):
    return [lax.ppermute(piece, AXES, perm) for piece, perm in zip(pieces, perms)]


def after(x, *others):
    return lax.optimization_barrier((x, *others))[0]


def per_device(tiles, tile_rows, tile_cols, counts, scaling):
    slots = tiles.shape[1]
    own = pack(tiles, tile_rows, tile_cols, counts, scaling)
    near = lax.ppermute(own, AXES, NEXT)
    own_same, own_cross, own_other = send([own] * 3, (SEND_SAME, SEND_CROSS, SWAP))
    own_dense = spread(own, own_other, slots)
    near_other = lax.ppermute(after(near, own_dense), AXES, SWAP)
    near_dense = spread(near, near_other, slots)
    near_same, near_cross = send((after(near, own_same), after(near, own_cross)), (SEND_SAME, SEND_CROSS))
    same, cross = [], []
    for pieces in ((own_same, near_same), (own_cross, near_cross)):
        kept, other = multiply((own_dense, near_dense), pieces, slots)
        same.append(lax.ppermute(kept, AXES, DONE_SAME))
        cross.append(lax.ppermute(other, AXES, DONE_CROSS))
    return join(*same, *cross)


def densify(tile_set, row_ids, col_ids, live_mask, scale_set, block_count):
    placed = jnp.zeros((block_count, RB, TB, TB), jnp.float32)
    placed = placed.at[col_ids, row_ids].add(tile_set * live_mask[:, None, None])
    placed = placed * scale_set[:, None, None, :]
    return placed.reshape(block_count, RB * TB, TB)


def place_panels(blocked, tile_set, row_ids, col_ids, live_mask, panel_count):
    picked = jnp.take(blocked, col_ids, axis=0)
    product = jnp.einsum("kac,kbc->kab", picked, tile_set, precision=lax.Precision.HIGHEST)
    product = product.reshape(panel_count, -1, RB * TB, TB)
    hit_row = (row_ids[:, None] == jnp.arange(RB, dtype=jnp.int32)[None, :]).astype(
        jnp.float32
    ) * live_mask[:, None]
    hit_row = hit_row.reshape(panel_count, -1, RB)
    placed = jnp.einsum("pkr,pkab->aprb", hit_row, product, precision=lax.Precision.HIGHEST)
    return placed.reshape(RB * TB, panel_count * RB * TB)


def per_device_any(tiles, tile_rows, tile_cols, counts, scaling):
    slot_total = tiles.shape[1]
    slot_range = jnp.arange(slot_total, dtype=jnp.int32)
    own_live = (slot_range < counts[0, 0]).astype(jnp.float32)
    blocked = densify(
        tiles[0], tile_rows[0], tile_cols[0], own_live, scaling.reshape(CB_DEV, TB), CB_DEV
    )
    piece_tiles = lax.all_gather(tiles, "rows", axis=0, tiled=True)
    piece_rows = lax.all_gather(tile_rows, "rows", axis=0, tiled=True)
    piece_cols = lax.all_gather(tile_cols, "rows", axis=0, tiled=True)
    piece_counts = lax.all_gather(counts, "rows", axis=0, tiled=True)
    count_here = piece_tiles.shape[0]
    live_mask = (slot_range[None, :] < piece_counts).astype(jnp.float32).reshape(-1)
    tile_block = place_panels(
        blocked,
        piece_tiles.reshape(count_here * slot_total, TB, TB),
        piece_rows.reshape(-1),
        piece_cols.reshape(-1),
        live_mask,
        count_here,
    )
    return lax.psum_scatter(tile_block, "cols", scatter_dimension=1, tiled=True)


def solution(mesh):
    placed = (
        P("rows", "cols", None, None),
        P("rows", "cols"),
        P("rows", "cols"),
        P("rows", "cols"),
        P("cols"),
    )
    small = mesh.shape["rows"] == 8 and mesh.shape["cols"] == 4
    return jax.shard_map(
        per_device if small else per_device_any,
        mesh=mesh,
        in_specs=placed,
        out_specs=P("rows", "cols"),
        check_vma=False,
    )
```

```python
import functools

import jax
import jax.numpy as jnp
from jax import lax
from jax.experimental import pallas as pl
from jax.experimental.pallas import tpu as pltpu
from jax.sharding import PartitionSpec as P

TB = 128
RB = 2
CB_DEV = 16
PANEL = RB * TB
META = 8
FEW = 5
AXES = ("rows", "cols")
VMEM_LIMIT = 16 * 1024 * 1024
PACK_LIMIT = 60 * 1024 * 1024
VSPEC = pl.BlockSpec(memory_space=pltpu.VMEM)
HSPEC = pl.BlockSpec(memory_space=pltpu.HBM)


def params(limit=VMEM_LIMIT):
    return pltpu.CompilerParams(vmem_limit_bytes=limit)


def cost(flops, nbytes):
    return pl.CostEstimate(flops=flops, bytes_accessed=nbytes, transcendentals=0)


def pack_kernel(slots, rows_hbm, cols_hbm, counts_hbm, tiles_hbm, scale_hbm, *refs):
    whole_ref, rows_ref, cols_ref, counts_ref, tiles_ref, scale_ref, sems = refs
    copies = [
        pltpu.make_async_copy(source, target, sems.at[index])
        for index, (source, target) in enumerate(
            (
                (rows_hbm, rows_ref),
                (cols_hbm, cols_ref),
                (counts_hbm, counts_ref),
                (scale_hbm, scale_ref),
                (tiles_hbm, tiles_ref),
            )
        )
    ]
    for copy in copies:
        copy.start()
    for copy in copies[:4]:
        copy.wait()
    lane = lax.broadcasted_iota(jnp.int32, (META, TB), 1)
    codes = jnp.full((META, TB), -1.0, jnp.float32)
    count = counts_ref[0, 0]
    factors = []
    for slot in range(slots):
        live = slot < count
        row = rows_ref[0, slot]
        col = cols_ref[0, slot]
        factors.append(jnp.where(live, jnp.sqrt(scale_ref[pl.ds(col, 1), :]), 0.0))
        code = jnp.where(live, col * RB + row, -1).astype(jnp.float32)
        codes = jnp.where(lane == slot, code, codes)
    copies[4].wait()
    for slot in range(slots):
        whole_ref[slot * TB : (slot + 1) * TB, :] = tiles_ref[0, slot] * factors[slot]
    whole_ref[slots * TB :, :] = codes


def pack(tiles, tile_rows, tile_cols, counts, scaling):
    slots = tiles.shape[1]
    return pl.pallas_call(
        functools.partial(pack_kernel, slots),
        out_shape=jax.ShapeDtypeStruct((slots * TB + META, TB), jnp.float32),
        in_specs=[HSPEC] * 5,
        out_specs=VSPEC,
        scratch_shapes=[
            pltpu.SMEM(tile_rows.shape, jnp.int32),
            pltpu.SMEM(tile_cols.shape, jnp.int32),
            pltpu.SMEM(counts.shape, jnp.int32),
            pltpu.VMEM(tiles.shape, jnp.float32),
            pltpu.VMEM((CB_DEV, TB), jnp.float32),
            pltpu.SemaphoreType.DMA((5,)),
        ],
        compiler_params=params(PACK_LIMIT),
        cost_estimate=cost(slots * TB * TB, 3 * slots * TB * TB * 4),
        name="pack",
    )(tile_rows, tile_cols, counts, tiles, scaling.reshape(CB_DEV, TB))


def read_codes(piece_ref, slots):
    row = piece_ref[slots * TB : slots * TB + META, :].astype(jnp.int32)
    return [row[0, slot] for slot in range(slots)]


def spread_kernel(slots, own_ref, other_ref, dense_ref, sum_ref, used_ref):
    codes = [read_codes(piece_ref, slots) for piece_ref in (own_ref, other_ref)]
    for col in range(CB_DEV):
        used_ref[col] = 0
    for side in range(2):
        for slot in range(slots):
            code = codes[side][slot]

            @pl.when(code >= 0)
            def _(code=code, slot=slot, side=side):
                col = code >> 1

                @pl.when(used_ref[col] == 0)
                def _():
                    used_ref[col] = 1
                    sum_ref[col] = jnp.zeros_like(sum_ref[col])

                start = pl.multiple_of(side * PANEL + (code & 1) * TB, TB)
                piece_ref = own_ref if side == 0 else other_ref
                sum_ref[col, pl.ds(start, TB), :] += piece_ref[slot * TB : (slot + 1) * TB, :]

    def convert(col, carry):
        @pl.when(used_ref[col] == 1)
        def _():
            high, low = split(sum_ref[col])
            dense_ref[col, :, :TB] = high
            dense_ref[col, :, TB:] = low

        @pl.when(used_ref[col] == 0)
        def _():
            dense_ref[col] = jnp.zeros_like(dense_ref[col])

        return carry

    lax.fori_loop(0, CB_DEV, convert, 0)


def spread(own, other, slots):
    return pl.pallas_call(
        functools.partial(spread_kernel, slots),
        out_shape=jax.ShapeDtypeStruct((CB_DEV, 2 * PANEL, 2 * TB), jnp.bfloat16),
        in_specs=[VSPEC] * 2,
        out_specs=VSPEC,
        scratch_shapes=[
            pltpu.VMEM((CB_DEV, 2 * PANEL, TB), jnp.float32),
            pltpu.SMEM((CB_DEV,), jnp.int32),
        ],
        compiler_params=params(),
        cost_estimate=cost(1 << 25, 1 << 25),
        name="spread",
    )(own, other)


def split(x):
    high = x.astype(jnp.bfloat16)
    low = (x - high.astype(jnp.float32)).astype(jnp.bfloat16)
    return high, low


def nt_dot(a, b):
    return lax.dot_general(a, b, (((1,), (1,)), ((), ())), preferred_element_type=jnp.float32)


def product(left, tile):
    high, low = split(tile)
    right = jnp.concatenate(
        [jnp.concatenate([high, high], axis=1), jnp.concatenate([low, low], axis=1)], axis=0
    )
    return nt_dot(left, right)


def for_tiles(slots, piece_refs, body):
    codes = [read_codes(piece_ref, slots) for piece_ref in piece_refs]

    def some(which, slot_range):
        for slot in slot_range:
            code = jnp.maximum(codes[which][slot], 0)
            body(which, slot, code >> 1, code & 1)

    few = min(FEW, slots)
    for which in range(len(piece_refs)):
        some(which, range(few))
    if few < slots:
        for which in range(len(piece_refs)):

            @pl.when(codes[which][few] >= 0)
            def _(which=which):
                some(which, range(few, slots))


def first_kernel(slots, dense_ref, *refs):
    count = len(refs) // 2
    piece_refs, acc_refs = refs[:count], refs[count:]
    for acc_ref in acc_refs:
        acc_ref[...] = jnp.zeros_like(acc_ref)

    def body(which, slot, col, block):
        both = product(dense_ref[col], piece_refs[which][slot * TB : (slot + 1) * TB, :])
        acc_refs[which][block] += both[:, :TB] + both[:, TB:]

    for_tiles(slots, piece_refs, body)


def first(dense, pieces, slots):
    return pl.pallas_call(
        functools.partial(first_kernel, slots),
        out_shape=[jax.ShapeDtypeStruct((RB, 2 * PANEL, TB), jnp.float32)] * len(pieces),
        in_specs=[VSPEC] * (1 + len(pieces)),
        out_specs=[VSPEC] * len(pieces),
        compiler_params=params(),
        cost_estimate=cost(1 << 25, 1 << 25),
        name="first",
    )(dense, *pieces)


def second_kernel(slots, dense_ref, acc_ref, piece_ref, kept_ref, other_ref, sum_ref):
    sum_ref[...] = acc_ref[...]

    def body(which, slot, col, block):
        both = product(dense_ref[col], piece_ref[slot * TB : (slot + 1) * TB, :])
        sum_ref[block] += both[:, :TB] + both[:, TB:]

    for_tiles(slots, (piece_ref,), body)
    for block in range(RB):
        lanes = slice(block * TB, (block + 1) * TB)
        kept_ref[:, lanes] = sum_ref[block, :PANEL, :]
        other_ref[:, lanes] = sum_ref[block, PANEL:, :]


def second(dense, acc, piece, slots):
    return pl.pallas_call(
        functools.partial(second_kernel, slots),
        out_shape=[jax.ShapeDtypeStruct((PANEL, PANEL), jnp.float32)] * 2,
        in_specs=[VSPEC] * 3,
        out_specs=[VSPEC] * 2,
        scratch_shapes=[pltpu.VMEM((RB, 2 * PANEL, TB), jnp.float32)],
        compiler_params=params(),
        cost_estimate=cost(1 << 25, 1 << 25),
        name="second",
    )(dense, acc, piece)


def join_kernel(cross_own_ref, cross_far_ref, same_own_ref, same_far_ref, out_ref):
    core = lax.axis_index("rows") & 1
    start = pl.multiple_of(core * PANEL, PANEL)
    out_ref[:, pl.ds(start, PANEL)] = same_own_ref[...] + cross_far_ref[...]
    out_ref[:, pl.ds(PANEL - start, PANEL)] = same_far_ref[...] + cross_own_ref[...]


def join(*results):
    return pl.pallas_call(
        join_kernel,
        out_shape=jax.ShapeDtypeStruct((PANEL, 2 * PANEL), jnp.float32),
        in_specs=[VSPEC] * 4,
        out_specs=VSPEC,
        compiler_params=params(),
        cost_estimate=cost(1 << 17, 1 << 17),
        name="join",
    )(*results)


def chunk(k, i, p):
    return k ^ p ^ (3 * (i ^ (p & 1) ^ (p >> 1)))


def pairs(place):
    out = []
    for row in range(8):
        for col in range(4):
            chip, core, plane = place(row >> 1, row & 1, col)
            out.append((row * 4 + col, (chip * 2 + core) * 4 + plane))
    return out


SWAP = pairs(lambda k, i, p: (k, 1 - i, p))
NEXT = pairs(lambda k, i, p: (k, i, p ^ 1))
SEND_SAME = pairs(lambda k, i, p: (chunk(k, i, p), i, p))
SEND_CROSS = pairs(lambda k, i, p: (chunk(k, 1 - i, p), 1 - i, p))
DONE_SAME = pairs(lambda k, i, p: (k, i, chunk(k, i, p)))
DONE_CROSS = pairs(lambda k, i, p: (k, 1 - i, chunk(k, i, p)))


def send(pieces, perms):
    return [lax.ppermute(piece, AXES, perm) for piece, perm in zip(pieces, perms)]


def after(x, *others):
    return lax.optimization_barrier((x, *others))[0]


def per_device(tiles, tile_rows, tile_cols, counts, scaling):
    slots = tiles.shape[1]
    own = pack(tiles, tile_rows, tile_cols, counts, scaling)
    near = lax.ppermute(own, AXES, NEXT)
    own_same, own_cross, own_other = send([own] * 3, (SEND_SAME, SEND_CROSS, SWAP))
    own_dense = spread(own, own_other, slots)
    near_other = lax.ppermute(after(near, own_dense), AXES, SWAP)
    near_dense = spread(near, near_other, slots)
    near_same, near_cross = send((after(near, own_same), after(near, own_cross)), (SEND_SAME, SEND_CROSS))
    accs = first(own_dense, (own_same, own_cross), slots)
    same, cross = [], []
    for acc, piece in zip(accs, (near_same, near_cross)):
        kept, other = second(near_dense, acc, piece, slots)
        same.append(lax.ppermute(kept, AXES, DONE_SAME))
        cross.append(lax.ppermute(other, AXES, DONE_CROSS))
    return join(cross[0], cross[1], same[0], same[1])


def densify(tile_set, row_ids, col_ids, live_mask, scale_set, block_count):
    placed = jnp.zeros((block_count, RB, TB, TB), jnp.float32)
    placed = placed.at[col_ids, row_ids].add(tile_set * live_mask[:, None, None])
    placed = placed * scale_set[:, None, None, :]
    return placed.reshape(block_count, RB * TB, TB)


def place_panels(blocked, tile_set, row_ids, col_ids, live_mask, panel_count):
    picked = jnp.take(blocked, col_ids, axis=0)
    product = jnp.einsum("kac,kbc->kab", picked, tile_set, precision=lax.Precision.HIGHEST)
    product = product.reshape(panel_count, -1, RB * TB, TB)
    hit_row = (row_ids[:, None] == jnp.arange(RB, dtype=jnp.int32)[None, :]).astype(
        jnp.float32
    ) * live_mask[:, None]
    hit_row = hit_row.reshape(panel_count, -1, RB)
    placed = jnp.einsum("pkr,pkab->aprb", hit_row, product, precision=lax.Precision.HIGHEST)
    return placed.reshape(RB * TB, panel_count * RB * TB)


def per_device_any(tiles, tile_rows, tile_cols, counts, scaling):
    slot_total = tiles.shape[1]
    slot_range = jnp.arange(slot_total, dtype=jnp.int32)
    own_live = (slot_range < counts[0, 0]).astype(jnp.float32)
    blocked = densify(
        tiles[0], tile_rows[0], tile_cols[0], own_live, scaling.reshape(CB_DEV, TB), CB_DEV
    )
    piece_tiles = lax.all_gather(tiles, "rows", axis=0, tiled=True)
    piece_rows = lax.all_gather(tile_rows, "rows", axis=0, tiled=True)
    piece_cols = lax.all_gather(tile_cols, "rows", axis=0, tiled=True)
    piece_counts = lax.all_gather(counts, "rows", axis=0, tiled=True)
    count_here = piece_tiles.shape[0]
    live_mask = (slot_range[None, :] < piece_counts).astype(jnp.float32).reshape(-1)
    tile_block = place_panels(
        blocked,
        piece_tiles.reshape(count_here * slot_total, TB, TB),
        piece_rows.reshape(-1),
        piece_cols.reshape(-1),
        live_mask,
        count_here,
    )
    return lax.psum_scatter(tile_block, "cols", scatter_dimension=1, tiled=True)


def solution(mesh):
    placed = (
        P("rows", "cols", None, None),
        P("rows", "cols"),
        P("rows", "cols"),
        P("rows", "cols"),
        P("cols"),
    )
    small = mesh.shape["rows"] == 8 and mesh.shape["cols"] == 4
    return jax.shard_map(
        per_device if small else per_device_any,
        mesh=mesh,
        in_specs=placed,
        out_specs=P("rows", "cols"),
        check_vma=False,
    )
```

```python
import functools

import jax
import jax.numpy as jnp
from jax import lax
from jax.experimental import pallas as pl
from jax.experimental.pallas import tpu as pltpu
from jax.sharding import PartitionSpec as P

TB = 128
RB = 2
CB_DEV = 16
PANEL = RB * TB
META = 8
FEW = 5
STEPS = 4
AXES = ("rows", "cols")
VMEM_LIMIT = 16 * 1024 * 1024
PACK_LIMIT = 60 * 1024 * 1024
VSPEC = pl.BlockSpec(memory_space=pltpu.VMEM)
HSPEC = pl.BlockSpec(memory_space=pltpu.HBM)


def params(limit=VMEM_LIMIT):
    return pltpu.CompilerParams(vmem_limit_bytes=limit)


def cost(flops, nbytes):
    return pl.CostEstimate(flops=flops, bytes_accessed=nbytes, transcendentals=0)


def pack_kernel(slots, rows_hbm, cols_hbm, counts_hbm, tiles_hbm, scale_hbm, whole_hbm, *scratch):
    rows_ref, cols_ref, counts_ref, scale_ref, tiles_ref, whole_ref, small_sems, in_sems, out_sems = scratch
    small = [
        pltpu.make_async_copy(source, target, small_sems.at[index])
        for index, (source, target) in enumerate(
            ((rows_hbm, rows_ref), (cols_hbm, cols_ref), (counts_hbm, counts_ref), (scale_hbm, scale_ref))
        )
    ]
    arrive = [
        pltpu.make_async_copy(tiles_hbm.at[0, slot], tiles_ref.at[slot], in_sems.at[slot])
        for slot in range(slots)
    ]
    for copy in small + arrive:
        copy.start()
    for copy in small:
        copy.wait()
    leave = []

    def send_rows(start, size):
        rows = pl.ds(start, size)
        copy = pltpu.make_async_copy(whole_ref.at[rows], whole_hbm.at[rows], out_sems.at[len(leave)])
        copy.start()
        leave.append(copy)

    lane = lax.broadcasted_iota(jnp.int32, (META, TB), 1)
    codes = jnp.full((META, TB), -1.0, jnp.float32)
    count = counts_ref[0, 0]
    for slot in range(slots):
        live = slot < count
        col = cols_ref[0, slot]
        code = jnp.where(live, col * RB + rows_ref[0, slot], -1).astype(jnp.float32)
        codes = jnp.where(lane == slot, code, codes)
        factor = jnp.where(live, jnp.sqrt(scale_ref[pl.ds(col, 1), :]), 0.0)
        arrive[slot].wait()
        whole_ref[slot * TB : (slot + 1) * TB, :] = tiles_ref[slot] * factor
        send_rows(slot * TB, TB)
    whole_ref[slots * TB :, :] = codes
    send_rows(slots * TB, META)
    for copy in leave:
        copy.wait()


def pack(tiles, tile_rows, tile_cols, counts, scaling):
    slots = tiles.shape[1]
    return pl.pallas_call(
        functools.partial(pack_kernel, slots),
        out_shape=jax.ShapeDtypeStruct((slots * TB + META, TB), jnp.float32),
        in_specs=[HSPEC] * 5,
        out_specs=HSPEC,
        scratch_shapes=[
            pltpu.SMEM(tile_rows.shape, jnp.int32),
            pltpu.SMEM(tile_cols.shape, jnp.int32),
            pltpu.SMEM(counts.shape, jnp.int32),
            pltpu.VMEM((CB_DEV, TB), jnp.float32),
            pltpu.VMEM((slots, TB, TB), jnp.float32),
            pltpu.VMEM((slots * TB + META, TB), jnp.float32),
            pltpu.SemaphoreType.DMA((4,)),
            pltpu.SemaphoreType.DMA((slots,)),
            pltpu.SemaphoreType.DMA((slots + 1,)),
        ],
        compiler_params=params(PACK_LIMIT),
        cost_estimate=cost(slots * TB * TB, 3 * slots * TB * TB * 4),
        name="pack",
    )(tile_rows, tile_cols, counts, tiles, scaling.reshape(CB_DEV, TB))


def read_codes(piece_ref, slots):
    row = piece_ref[slots * TB : slots * TB + META, :].astype(jnp.int32)
    return [row[0, slot] for slot in range(slots)]


def spread_kernel(slots, own_ref, other_ref, dense_ref, sum_ref, used_ref):
    codes = [read_codes(piece_ref, slots) for piece_ref in (own_ref, other_ref)]
    for col in range(CB_DEV):
        used_ref[col] = 0
    for side in range(2):
        for slot in range(slots):
            code = codes[side][slot]

            @pl.when(code >= 0)
            def _(code=code, slot=slot, side=side):
                col = code >> 1

                @pl.when(used_ref[col] == 0)
                def _():
                    used_ref[col] = 1
                    sum_ref[col] = jnp.zeros_like(sum_ref[col])

                start = pl.multiple_of(side * PANEL + (code & 1) * TB, TB)
                piece_ref = own_ref if side == 0 else other_ref
                sum_ref[col, pl.ds(start, TB), :] += piece_ref[slot * TB : (slot + 1) * TB, :]

    def convert(col, carry):
        @pl.when(used_ref[col] == 1)
        def _():
            high, low = split(sum_ref[col])
            dense_ref[col, :, :TB] = high
            dense_ref[col, :, TB:] = low

        @pl.when(used_ref[col] == 0)
        def _():
            dense_ref[col] = jnp.zeros_like(dense_ref[col])

        return carry

    lax.fori_loop(0, CB_DEV, convert, 0)


def spread(own, other, slots):
    return pl.pallas_call(
        functools.partial(spread_kernel, slots),
        out_shape=jax.ShapeDtypeStruct((CB_DEV, 2 * PANEL, 2 * TB), jnp.bfloat16),
        in_specs=[VSPEC] * 2,
        out_specs=VSPEC,
        scratch_shapes=[
            pltpu.VMEM((CB_DEV, 2 * PANEL, TB), jnp.float32),
            pltpu.SMEM((CB_DEV,), jnp.int32),
        ],
        compiler_params=params(),
        cost_estimate=cost(1 << 25, 1 << 25),
        name="spread",
    )(own, other)


def split(x):
    high = x.astype(jnp.bfloat16)
    low = (x - high.astype(jnp.float32)).astype(jnp.bfloat16)
    return high, low


def nt_dot(a, b):
    return lax.dot_general(a, b, (((1,), (1,)), ((), ())), preferred_element_type=jnp.float32)


def product(left, tile):
    high, low = split(tile)
    right = jnp.concatenate(
        [jnp.concatenate([high, high], axis=1), jnp.concatenate([low, low], axis=1)], axis=0
    )
    return nt_dot(left, right)


def for_tiles(slots, piece_refs, body):
    codes = [read_codes(piece_ref, slots) for piece_ref in piece_refs]

    def some(which, slot_range):
        for slot in slot_range:
            code = jnp.maximum(codes[which][slot], 0)
            body(which, slot, code >> 1, code & 1)

    few = min(FEW, slots)
    for which in range(len(piece_refs)):
        some(which, range(few))
    if few < slots:
        for which in range(len(piece_refs)):

            @pl.when(codes[which][few] >= 0)
            def _(which=which):
                some(which, range(few, slots))


def first_kernel(slots, dense_ref, *refs):
    count = len(refs) // 2
    piece_refs, acc_refs = refs[:count], refs[count:]
    for acc_ref in acc_refs:
        acc_ref[...] = jnp.zeros_like(acc_ref)

    def body(which, slot, col, block):
        both = product(dense_ref[col], piece_refs[which][slot * TB : (slot + 1) * TB, :])
        acc_refs[which][block] += both[:, :TB] + both[:, TB:]

    for_tiles(slots, piece_refs, body)


def first(dense, pieces, slots):
    return pl.pallas_call(
        functools.partial(first_kernel, slots),
        out_shape=[jax.ShapeDtypeStruct((RB, 2 * PANEL, TB), jnp.float32)] * len(pieces),
        in_specs=[VSPEC] * (1 + len(pieces)),
        out_specs=[VSPEC] * len(pieces),
        compiler_params=params(),
        cost_estimate=cost(1 << 25, 1 << 25),
        name="first",
    )(dense, *pieces)


def second_kernel(slots, dense_ref, acc_ref, piece_ref, kept_ref, other_ref, sum_ref):
    sum_ref[...] = acc_ref[...]

    def body(which, slot, col, block):
        both = product(dense_ref[col], piece_ref[slot * TB : (slot + 1) * TB, :])
        sum_ref[block] += both[:, :TB] + both[:, TB:]

    for_tiles(slots, (piece_ref,), body)
    for block in range(RB):
        lanes = slice(block * TB, (block + 1) * TB)
        kept_ref[:, lanes] = sum_ref[block, :PANEL, :]
        other_ref[:, lanes] = sum_ref[block, PANEL:, :]


def second(dense, acc, piece, slots):
    return pl.pallas_call(
        functools.partial(second_kernel, slots),
        out_shape=[jax.ShapeDtypeStruct((PANEL, PANEL), jnp.float32)] * 2,
        in_specs=[VSPEC] * 3,
        out_specs=[VSPEC] * 2,
        scratch_shapes=[pltpu.VMEM((RB, 2 * PANEL, TB), jnp.float32)],
        compiler_params=params(),
        cost_estimate=cost(1 << 25, 1 << 25),
        name="second",
    )(dense, acc, piece)


def join_kernel(cross_own_ref, cross_far_ref, same_own_ref, same_far_ref, out_hbm, out_ref, sems):
    core = lax.axis_index("rows") & 1
    start = pl.multiple_of(core * PANEL, PANEL)
    size = PANEL // STEPS
    copies = []
    for step in range(STEPS):
        rows = pl.ds(step * size, size)
        out_ref[rows, pl.ds(start, PANEL)] = same_own_ref[rows, :] + cross_far_ref[rows, :]
        out_ref[rows, pl.ds(PANEL - start, PANEL)] = same_far_ref[rows, :] + cross_own_ref[rows, :]
        copies.append(pltpu.make_async_copy(out_ref.at[rows], out_hbm.at[rows], sems.at[step]))
        copies[-1].start()
    for copy in copies:
        copy.wait()


def join(*results):
    shape = (PANEL, 2 * PANEL)
    return pl.pallas_call(
        join_kernel,
        out_shape=jax.ShapeDtypeStruct(shape, jnp.float32),
        in_specs=[VSPEC] * 4,
        out_specs=HSPEC,
        scratch_shapes=[pltpu.VMEM(shape, jnp.float32), pltpu.SemaphoreType.DMA((STEPS,))],
        compiler_params=params(),
        cost_estimate=cost(1 << 17, 1 << 17),
        name="join",
    )(*results)


def chunk(k, i, p):
    return k ^ p ^ (3 * (i ^ (p & 1) ^ (p >> 1)))


def pairs(place):
    out = []
    for row in range(8):
        for col in range(4):
            chip, core, plane = place(row >> 1, row & 1, col)
            out.append((row * 4 + col, (chip * 2 + core) * 4 + plane))
    return out


SWAP = pairs(lambda k, i, p: (k, 1 - i, p))
NEXT = pairs(lambda k, i, p: (k, i, p ^ 1))
SEND_SAME = pairs(lambda k, i, p: (chunk(k, i, p), i, p))
SEND_CROSS = pairs(lambda k, i, p: (chunk(k, 1 - i, p), 1 - i, p))
DONE_SAME = pairs(lambda k, i, p: (k, i, chunk(k, i, p)))
DONE_CROSS = pairs(lambda k, i, p: (k, 1 - i, chunk(k, i, p)))


def send(pieces, perms):
    return [lax.ppermute(piece, AXES, perm) for piece, perm in zip(pieces, perms)]


def after(x, *others):
    return lax.optimization_barrier((x, *others))[0]


def per_device(tiles, tile_rows, tile_cols, counts, scaling):
    slots = tiles.shape[1]
    own = pack(tiles, tile_rows, tile_cols, counts, scaling)
    near = lax.ppermute(own, AXES, NEXT)
    own_same, own_cross, own_other = send([own] * 3, (SEND_SAME, SEND_CROSS, SWAP))
    own_dense = spread(own, own_other, slots)
    near_other = lax.ppermute(after(near, own_dense), AXES, SWAP)
    near_dense = spread(near, near_other, slots)
    near_same, near_cross = send((after(near, own_same), after(near, own_cross)), (SEND_SAME, SEND_CROSS))
    accs = first(own_dense, (own_same, own_cross), slots)
    same, cross = [], []
    for acc, piece in zip(accs, (near_same, near_cross)):
        kept, other = second(near_dense, acc, piece, slots)
        same.append(lax.ppermute(kept, AXES, DONE_SAME))
        cross.append(lax.ppermute(other, AXES, DONE_CROSS))
    return join(cross[0], cross[1], same[0], same[1])


def densify(tile_set, row_ids, col_ids, live_mask, scale_set, block_count):
    placed = jnp.zeros((block_count, RB, TB, TB), jnp.float32)
    placed = placed.at[col_ids, row_ids].add(tile_set * live_mask[:, None, None])
    placed = placed * scale_set[:, None, None, :]
    return placed.reshape(block_count, RB * TB, TB)


def place_panels(blocked, tile_set, row_ids, col_ids, live_mask, panel_count):
    picked = jnp.take(blocked, col_ids, axis=0)
    product = jnp.einsum("kac,kbc->kab", picked, tile_set, precision=lax.Precision.HIGHEST)
    product = product.reshape(panel_count, -1, RB * TB, TB)
    hit_row = (row_ids[:, None] == jnp.arange(RB, dtype=jnp.int32)[None, :]).astype(
        jnp.float32
    ) * live_mask[:, None]
    hit_row = hit_row.reshape(panel_count, -1, RB)
    placed = jnp.einsum("pkr,pkab->aprb", hit_row, product, precision=lax.Precision.HIGHEST)
    return placed.reshape(RB * TB, panel_count * RB * TB)


def per_device_any(tiles, tile_rows, tile_cols, counts, scaling):
    slot_total = tiles.shape[1]
    slot_range = jnp.arange(slot_total, dtype=jnp.int32)
    own_live = (slot_range < counts[0, 0]).astype(jnp.float32)
    blocked = densify(
        tiles[0], tile_rows[0], tile_cols[0], own_live, scaling.reshape(CB_DEV, TB), CB_DEV
    )
    piece_tiles = lax.all_gather(tiles, "rows", axis=0, tiled=True)
    piece_rows = lax.all_gather(tile_rows, "rows", axis=0, tiled=True)
    piece_cols = lax.all_gather(tile_cols, "rows", axis=0, tiled=True)
    piece_counts = lax.all_gather(counts, "rows", axis=0, tiled=True)
    count_here = piece_tiles.shape[0]
    live_mask = (slot_range[None, :] < piece_counts).astype(jnp.float32).reshape(-1)
    tile_block = place_panels(
        blocked,
        piece_tiles.reshape(count_here * slot_total, TB, TB),
        piece_rows.reshape(-1),
        piece_cols.reshape(-1),
        live_mask,
        count_here,
    )
    return lax.psum_scatter(tile_block, "cols", scatter_dimension=1, tiled=True)


def solution(mesh):
    placed = (
        P("rows", "cols", None, None),
        P("rows", "cols"),
        P("rows", "cols"),
        P("rows", "cols"),
        P("cols"),
    )
    small = mesh.shape["rows"] == 8 and mesh.shape["cols"] == 4
    return jax.shard_map(
        per_device if small else per_device_any,
        mesh=mesh,
        in_specs=placed,
        out_specs=P("rows", "cols"),
        check_vma=False,
    )
```

```python
import functools

import jax
import jax.numpy as jnp
from jax import lax
from jax.experimental import pallas as pl
from jax.experimental.pallas import tpu as pltpu
from jax.sharding import PartitionSpec as P

TB = 128
RB = 2
CB_DEV = 16
PANEL = RB * TB
META = 8
FEW = 5
STEPS = 4
AXES = ("rows", "cols")
VMEM_LIMIT = 16 * 1024 * 1024
PACK_LIMIT = 60 * 1024 * 1024
VSPEC = pl.BlockSpec(memory_space=pltpu.VMEM)
HSPEC = pl.BlockSpec(memory_space=pltpu.HBM)


def params(limit=VMEM_LIMIT):
    return pltpu.CompilerParams(vmem_limit_bytes=limit)


def cost(flops, nbytes):
    return pl.CostEstimate(flops=flops, bytes_accessed=nbytes, transcendentals=0)


def pack_kernel(slots, rows_hbm, cols_hbm, counts_hbm, tiles_hbm, scale_hbm, whole_hbm, *scratch):
    rows_ref, cols_ref, counts_ref, scale_ref, tiles_ref, whole_ref, small_sems, in_sems, out_sems = scratch
    small = [
        pltpu.make_async_copy(source, target, small_sems.at[index])
        for index, (source, target) in enumerate(
            ((rows_hbm, rows_ref), (cols_hbm, cols_ref), (counts_hbm, counts_ref), (scale_hbm, scale_ref))
        )
    ]
    arrive = [
        pltpu.make_async_copy(tiles_hbm.at[0, slot], tiles_ref.at[slot], in_sems.at[slot])
        for slot in range(slots)
    ]
    for copy in small + arrive:
        copy.start()
    for copy in small:
        copy.wait()
    leave = []

    def send_rows(start, size):
        rows = pl.ds(start, size)
        copy = pltpu.make_async_copy(whole_ref.at[rows], whole_hbm.at[rows], out_sems.at[len(leave)])
        copy.start()
        leave.append(copy)

    lane = lax.broadcasted_iota(jnp.int32, (META, TB), 1)
    codes = jnp.full((META, TB), -1.0, jnp.float32)
    count = counts_ref[0, 0]
    for slot in range(slots):
        live = slot < count
        col = cols_ref[0, slot]
        code = jnp.where(live, col * RB + rows_ref[0, slot], -1).astype(jnp.float32)
        codes = jnp.where(lane == slot, code, codes)
        factor = jnp.where(live, jnp.sqrt(scale_ref[pl.ds(col, 1), :]), 0.0)
        arrive[slot].wait()
        whole_ref[slot * TB : (slot + 1) * TB, :] = tiles_ref[slot] * factor
        send_rows(slot * TB, TB)
    whole_ref[slots * TB :, :] = codes
    send_rows(slots * TB, META)
    for copy in leave:
        copy.wait()


def pack(tiles, tile_rows, tile_cols, counts, scaling):
    slots = tiles.shape[1]
    return pl.pallas_call(
        functools.partial(pack_kernel, slots),
        out_shape=jax.ShapeDtypeStruct((slots * TB + META, TB), jnp.float32),
        in_specs=[HSPEC] * 5,
        out_specs=HSPEC,
        scratch_shapes=[
            pltpu.SMEM(tile_rows.shape, jnp.int32),
            pltpu.SMEM(tile_cols.shape, jnp.int32),
            pltpu.SMEM(counts.shape, jnp.int32),
            pltpu.VMEM((CB_DEV, TB), jnp.float32),
            pltpu.VMEM((slots, TB, TB), jnp.float32),
            pltpu.VMEM((slots * TB + META, TB), jnp.float32),
            pltpu.SemaphoreType.DMA((4,)),
            pltpu.SemaphoreType.DMA((slots,)),
            pltpu.SemaphoreType.DMA((slots + 1,)),
        ],
        compiler_params=params(PACK_LIMIT),
        cost_estimate=cost(slots * TB * TB, 3 * slots * TB * TB * 4),
        name="pack",
    )(tile_rows, tile_cols, counts, tiles, scaling.reshape(CB_DEV, TB))


def read_codes(piece_ref, slots):
    row = piece_ref[slots * TB : slots * TB + META, :].astype(jnp.int32)
    return [row[0, slot] for slot in range(slots)]


def spread_kernel(slots, own_ref, other_ref, dense_ref, sum_ref, used_ref):
    codes = [read_codes(piece_ref, slots) for piece_ref in (own_ref, other_ref)]
    for col in range(CB_DEV):
        used_ref[col] = 0
    for side in range(2):
        for slot in range(slots):
            code = codes[side][slot]

            @pl.when(code >= 0)
            def _(code=code, slot=slot, side=side):
                col = code >> 1

                @pl.when(used_ref[col] == 0)
                def _():
                    used_ref[col] = 1
                    sum_ref[col] = jnp.zeros_like(sum_ref[col])

                start = pl.multiple_of(side * PANEL + (code & 1) * TB, TB)
                piece_ref = own_ref if side == 0 else other_ref
                sum_ref[col, pl.ds(start, TB), :] += piece_ref[slot * TB : (slot + 1) * TB, :]

    def convert(col, carry):
        @pl.when(used_ref[col] == 1)
        def _():
            high, low = split(sum_ref[col])
            dense_ref[col, :, :TB] = high
            dense_ref[col, :, TB:] = low

        @pl.when(used_ref[col] == 0)
        def _():
            dense_ref[col] = jnp.zeros_like(dense_ref[col])

        return carry

    lax.fori_loop(0, CB_DEV, convert, 0)


def spread(own, other, slots):
    return pl.pallas_call(
        functools.partial(spread_kernel, slots),
        out_shape=jax.ShapeDtypeStruct((CB_DEV, 2 * PANEL, 2 * TB), jnp.bfloat16),
        in_specs=[VSPEC] * 2,
        out_specs=VSPEC,
        scratch_shapes=[
            pltpu.VMEM((CB_DEV, 2 * PANEL, TB), jnp.float32),
            pltpu.SMEM((CB_DEV,), jnp.int32),
        ],
        compiler_params=params(),
        cost_estimate=cost(1 << 25, 1 << 25),
        name="spread",
    )(own, other)


def split(x):
    high = x.astype(jnp.bfloat16)
    low = (x - high.astype(jnp.float32)).astype(jnp.bfloat16)
    return high, low


def nt_dot(a, b):
    return lax.dot_general(a, b, (((1,), (1,)), ((), ())), preferred_element_type=jnp.float32)


def product(left, tile):
    high, low = split(tile)
    right = jnp.concatenate(
        [jnp.concatenate([high, high], axis=1), jnp.concatenate([low, low], axis=1)], axis=0
    )
    return nt_dot(left, right)


def for_tiles(slots, piece_refs, body):
    codes = [read_codes(piece_ref, slots) for piece_ref in piece_refs]

    def some(which, slot_range):
        for slot in slot_range:
            code = jnp.maximum(codes[which][slot], 0)
            body(which, slot, code >> 1, code & 1)

    few = min(FEW, slots)
    for which in range(len(piece_refs)):
        some(which, range(few))
    if few < slots:
        for which in range(len(piece_refs)):

            @pl.when(codes[which][few] >= 0)
            def _(which=which):
                some(which, range(few, slots))


def first_kernel(slots, dense_ref, *refs):
    count = len(refs) // 2
    piece_refs, acc_refs = refs[:count], refs[count:]
    for acc_ref in acc_refs:
        acc_ref[...] = jnp.zeros_like(acc_ref)

    def body(which, slot, col, block):
        both = product(dense_ref[col], piece_refs[which][slot * TB : (slot + 1) * TB, :])
        acc_refs[which][block] += both[:, :TB] + both[:, TB:]

    for_tiles(slots, piece_refs, body)


def first(dense, pieces, slots):
    return pl.pallas_call(
        functools.partial(first_kernel, slots),
        out_shape=[jax.ShapeDtypeStruct((RB, 2 * PANEL, TB), jnp.float32)] * len(pieces),
        in_specs=[VSPEC] * (1 + len(pieces)),
        out_specs=[VSPEC] * len(pieces),
        compiler_params=params(),
        cost_estimate=cost(1 << 25, 1 << 25),
        name="first",
    )(dense, *pieces)


def second_kernel(slots, dense_ref, acc_ref, piece_ref, kept_ref, other_ref, sum_ref):
    sum_ref[...] = acc_ref[...]

    def body(which, slot, col, block):
        both = product(dense_ref[col], piece_ref[slot * TB : (slot + 1) * TB, :])
        sum_ref[block] += both[:, :TB] + both[:, TB:]

    for_tiles(slots, (piece_ref,), body)
    for block in range(RB):
        lanes = slice(block * TB, (block + 1) * TB)
        kept_ref[:, lanes] = sum_ref[block, :PANEL, :]
        other_ref[:, lanes] = sum_ref[block, PANEL:, :]


def second(dense, acc, piece, slots):
    return pl.pallas_call(
        functools.partial(second_kernel, slots),
        out_shape=[jax.ShapeDtypeStruct((PANEL, PANEL), jnp.float32)] * 2,
        in_specs=[VSPEC] * 3,
        out_specs=[VSPEC] * 2,
        scratch_shapes=[pltpu.VMEM((RB, 2 * PANEL, TB), jnp.float32)],
        compiler_params=params(),
        cost_estimate=cost(1 << 25, 1 << 25),
        name="second",
    )(dense, acc, piece)


def join_kernel(same_own_ref, cross_own_ref, cross_far_ref, same_far_ref, out_hbm, out_ref, sems):
    core = lax.axis_index("rows") & 1
    start = pl.multiple_of(core * PANEL, PANEL)
    size = PANEL // STEPS
    copies = []
    for step in range(STEPS):
        rows = pl.ds(step * size, size)
        out_ref[rows, pl.ds(start, PANEL)] = same_own_ref[rows, :] + cross_far_ref[rows, :]
        out_ref[rows, pl.ds(PANEL - start, PANEL)] = same_far_ref[rows, :] + cross_own_ref[rows, :]
        copies.append(pltpu.make_async_copy(out_ref.at[rows], out_hbm.at[rows], sems.at[step]))
        copies[-1].start()
    for copy in copies:
        copy.wait()


def join(*results):
    shape = (PANEL, 2 * PANEL)
    return pl.pallas_call(
        join_kernel,
        out_shape=jax.ShapeDtypeStruct(shape, jnp.float32),
        in_specs=[VSPEC] * 4,
        out_specs=HSPEC,
        scratch_shapes=[pltpu.VMEM(shape, jnp.float32), pltpu.SemaphoreType.DMA((STEPS,))],
        compiler_params=params(),
        cost_estimate=cost(1 << 17, 1 << 17),
        name="join",
    )(*results)


def chunk(k, i, p):
    return k ^ p ^ (3 * (i ^ (p & 1) ^ (p >> 1)))


def pairs(place):
    out = []
    for row in range(8):
        for col in range(4):
            chip, core, plane = place(row >> 1, row & 1, col)
            out.append((row * 4 + col, (chip * 2 + core) * 4 + plane))
    return out


SWAP = pairs(lambda k, i, p: (k, 1 - i, p))
NEXT = pairs(lambda k, i, p: (k, i, p ^ 1))
SEND_SAME = pairs(lambda k, i, p: (chunk(k, i, p), i, p))
SEND_CROSS = pairs(lambda k, i, p: (chunk(k, 1 - i, p), 1 - i, p))
DONE_SAME = pairs(lambda k, i, p: (k, i, chunk(k, i, p)))
DONE_CROSS = pairs(lambda k, i, p: (k, 1 - i, chunk(k, i, p)))


def send(pieces, perms):
    return [lax.ppermute(piece, AXES, perm) for piece, perm in zip(pieces, perms)]


def after(x, *others):
    return lax.optimization_barrier((x, *others))[0]


def per_device(tiles, tile_rows, tile_cols, counts, scaling):
    slots = tiles.shape[1]
    own = pack(tiles, tile_rows, tile_cols, counts, scaling)
    near = lax.ppermute(own, AXES, NEXT)
    own_same, own_cross, own_other = send([own] * 3, (SEND_SAME, SEND_CROSS, SWAP))
    own_dense = spread(own, own_other, slots)
    near_other = lax.ppermute(after(near, own_dense), AXES, SWAP)
    near_dense = spread(near, near_other, slots)
    near_same, near_cross = send((after(near, own_same), after(near, own_cross)), (SEND_SAME, SEND_CROSS))
    accs = first(own_dense, (own_same, own_cross), slots)
    same, cross = [], []
    for acc, piece in zip(accs, (near_same, near_cross)):
        kept, other = second(near_dense, acc, piece, slots)
        same.append(lax.ppermute(kept, AXES, DONE_SAME))
        cross.append(lax.ppermute(other, AXES, DONE_CROSS))
    return join(same[0], cross[0], cross[1], same[1])


def densify(tile_set, row_ids, col_ids, live_mask, scale_set, block_count):
    placed = jnp.zeros((block_count, RB, TB, TB), jnp.float32)
    placed = placed.at[col_ids, row_ids].add(tile_set * live_mask[:, None, None])
    placed = placed * scale_set[:, None, None, :]
    return placed.reshape(block_count, RB * TB, TB)


def place_panels(blocked, tile_set, row_ids, col_ids, live_mask, panel_count):
    picked = jnp.take(blocked, col_ids, axis=0)
    product = jnp.einsum("kac,kbc->kab", picked, tile_set, precision=lax.Precision.HIGHEST)
    product = product.reshape(panel_count, -1, RB * TB, TB)
    hit_row = (row_ids[:, None] == jnp.arange(RB, dtype=jnp.int32)[None, :]).astype(
        jnp.float32
    ) * live_mask[:, None]
    hit_row = hit_row.reshape(panel_count, -1, RB)
    placed = jnp.einsum("pkr,pkab->aprb", hit_row, product, precision=lax.Precision.HIGHEST)
    return placed.reshape(RB * TB, panel_count * RB * TB)


def per_device_any(tiles, tile_rows, tile_cols, counts, scaling):
    slot_total = tiles.shape[1]
    slot_range = jnp.arange(slot_total, dtype=jnp.int32)
    own_live = (slot_range < counts[0, 0]).astype(jnp.float32)
    blocked = densify(
        tiles[0], tile_rows[0], tile_cols[0], own_live, scaling.reshape(CB_DEV, TB), CB_DEV
    )
    piece_tiles = lax.all_gather(tiles, "rows", axis=0, tiled=True)
    piece_rows = lax.all_gather(tile_rows, "rows", axis=0, tiled=True)
    piece_cols = lax.all_gather(tile_cols, "rows", axis=0, tiled=True)
    piece_counts = lax.all_gather(counts, "rows", axis=0, tiled=True)
    count_here = piece_tiles.shape[0]
    live_mask = (slot_range[None, :] < piece_counts).astype(jnp.float32).reshape(-1)
    tile_block = place_panels(
        blocked,
        piece_tiles.reshape(count_here * slot_total, TB, TB),
        piece_rows.reshape(-1),
        piece_cols.reshape(-1),
        live_mask,
        count_here,
    )
    return lax.psum_scatter(tile_block, "cols", scatter_dimension=1, tiled=True)


def solution(mesh):
    placed = (
        P("rows", "cols", None, None),
        P("rows", "cols"),
        P("rows", "cols"),
        P("rows", "cols"),
        P("cols"),
    )
    small = mesh.shape["rows"] == 8 and mesh.shape["cols"] == 4
    return jax.shard_map(
        per_device if small else per_device_any,
        mesh=mesh,
        in_specs=placed,
        out_specs=P("rows", "cols"),
        check_vma=False,
    )
```

```python
import functools

import jax
import jax.numpy as jnp
from jax import lax
from jax.experimental import pallas as pl
from jax.experimental.pallas import tpu as pltpu
from jax.sharding import PartitionSpec as P

TB = 128
RB = 2
CB_DEV = 16
PANEL = RB * TB
META = 8
FEW = 8
STEPS = 4
AXES = ("rows", "cols")
VMEM_LIMIT = 16 * 1024 * 1024
PACK_LIMIT = 60 * 1024 * 1024
VSPEC = pl.BlockSpec(memory_space=pltpu.VMEM)
HSPEC = pl.BlockSpec(memory_space=pltpu.HBM)


def params(limit=VMEM_LIMIT):
    return pltpu.CompilerParams(vmem_limit_bytes=limit)


def cost(flops, nbytes):
    return pl.CostEstimate(flops=flops, bytes_accessed=nbytes, transcendentals=0)


def pack_kernel(slots, rows_hbm, cols_hbm, counts_hbm, tiles_hbm, scale_hbm, whole_hbm, *scratch):
    rows_ref, cols_ref, counts_ref, scale_ref, tiles_ref, whole_ref, small_sems, in_sems, out_sems = scratch
    small = [
        pltpu.make_async_copy(source, target, small_sems.at[index])
        for index, (source, target) in enumerate(
            ((rows_hbm, rows_ref), (cols_hbm, cols_ref), (counts_hbm, counts_ref), (scale_hbm, scale_ref))
        )
    ]
    arrive = [
        pltpu.make_async_copy(tiles_hbm.at[0, slot], tiles_ref.at[slot], in_sems.at[slot])
        for slot in range(slots)
    ]
    for copy in small + arrive:
        copy.start()
    for copy in small:
        copy.wait()
    leave = []

    def send_rows(start, size):
        rows = pl.ds(start, size)
        copy = pltpu.make_async_copy(whole_ref.at[rows], whole_hbm.at[rows], out_sems.at[len(leave)])
        copy.start()
        leave.append(copy)

    lane = lax.broadcasted_iota(jnp.int32, (META, TB), 1)
    codes = jnp.full((META, TB), -1.0, jnp.float32)
    count = counts_ref[0, 0]
    for slot in range(slots):
        live = slot < count
        col = cols_ref[0, slot]
        code = jnp.where(live, col * RB + rows_ref[0, slot], -1).astype(jnp.float32)
        codes = jnp.where(lane == slot, code, codes)
        factor = jnp.where(live, jnp.sqrt(scale_ref[pl.ds(col, 1), :]), 0.0)
        arrive[slot].wait()
        whole_ref[slot * TB : (slot + 1) * TB, :] = tiles_ref[slot] * factor
        send_rows(slot * TB, TB)
    whole_ref[slots * TB :, :] = codes
    send_rows(slots * TB, META)
    for copy in leave:
        copy.wait()


def pack(tiles, tile_rows, tile_cols, counts, scaling):
    slots = tiles.shape[1]
    return pl.pallas_call(
        functools.partial(pack_kernel, slots),
        out_shape=jax.ShapeDtypeStruct((slots * TB + META, TB), jnp.float32),
        in_specs=[HSPEC] * 5,
        out_specs=HSPEC,
        scratch_shapes=[
            pltpu.SMEM(tile_rows.shape, jnp.int32),
            pltpu.SMEM(tile_cols.shape, jnp.int32),
            pltpu.SMEM(counts.shape, jnp.int32),
            pltpu.VMEM((CB_DEV, TB), jnp.float32),
            pltpu.VMEM((slots, TB, TB), jnp.float32),
            pltpu.VMEM((slots * TB + META, TB), jnp.float32),
            pltpu.SemaphoreType.DMA((4,)),
            pltpu.SemaphoreType.DMA((slots,)),
            pltpu.SemaphoreType.DMA((slots + 1,)),
        ],
        compiler_params=params(PACK_LIMIT),
        cost_estimate=cost(slots * TB * TB, 3 * slots * TB * TB * 4),
        name="pack",
    )(tile_rows, tile_cols, counts, tiles, scaling.reshape(CB_DEV, TB))


def read_codes(piece_ref, slots):
    row = piece_ref[slots * TB : slots * TB + META, :].astype(jnp.int32)
    return [row[0, slot] for slot in range(slots)]


def spread_kernel(slots, own_ref, other_ref, dense_ref, sum_ref, used_ref):
    codes = [read_codes(piece_ref, slots) for piece_ref in (own_ref, other_ref)]
    for col in range(CB_DEV):
        used_ref[col] = 0
    for side in range(2):
        for slot in range(slots):
            code = codes[side][slot]

            @pl.when(code >= 0)
            def _(code=code, slot=slot, side=side):
                col = code >> 1

                @pl.when(used_ref[col] == 0)
                def _():
                    used_ref[col] = 1
                    sum_ref[col] = jnp.zeros_like(sum_ref[col])

                start = pl.multiple_of(side * PANEL + (code & 1) * TB, TB)
                piece_ref = own_ref if side == 0 else other_ref
                sum_ref[col, pl.ds(start, TB), :] += piece_ref[slot * TB : (slot + 1) * TB, :]

    def convert(col, carry):
        @pl.when(used_ref[col] == 1)
        def _():
            high, low = split(sum_ref[col])
            dense_ref[col, :, :TB] = high
            dense_ref[col, :, TB:] = low

        @pl.when(used_ref[col] == 0)
        def _():
            dense_ref[col] = jnp.zeros_like(dense_ref[col])

        return carry

    lax.fori_loop(0, CB_DEV, convert, 0)


def spread(own, other, slots):
    return pl.pallas_call(
        functools.partial(spread_kernel, slots),
        out_shape=jax.ShapeDtypeStruct((CB_DEV, 2 * PANEL, 2 * TB), jnp.bfloat16),
        in_specs=[VSPEC] * 2,
        out_specs=VSPEC,
        scratch_shapes=[
            pltpu.VMEM((CB_DEV, 2 * PANEL, TB), jnp.float32),
            pltpu.SMEM((CB_DEV,), jnp.int32),
        ],
        compiler_params=params(),
        cost_estimate=cost(1 << 25, 1 << 25),
        name="spread",
    )(own, other)


def split(x):
    high = x.astype(jnp.bfloat16)
    low = (x - high.astype(jnp.float32)).astype(jnp.bfloat16)
    return high, low


def nt_dot(a, b):
    return lax.dot_general(a, b, (((1,), (1,)), ((), ())), preferred_element_type=jnp.float32)


def product(left, tile):
    high, low = split(tile)
    right = jnp.concatenate(
        [jnp.concatenate([high, high], axis=1), jnp.concatenate([low, low], axis=1)], axis=0
    )
    return nt_dot(left, right)


def for_tiles(slots, piece_refs, body):
    codes = [read_codes(piece_ref, slots) for piece_ref in piece_refs]

    def some(which, slot_range):
        for slot in slot_range:
            code = jnp.maximum(codes[which][slot], 0)
            body(which, slot, code >> 1, code & 1)

    few = min(FEW, slots)
    for which in range(len(piece_refs)):
        some(which, range(few))
    if few < slots:
        for which in range(len(piece_refs)):

            @pl.when(codes[which][few] >= 0)
            def _(which=which):
                some(which, range(few, slots))


def first_kernel(slots, dense_ref, *refs):
    count = len(refs) // 2
    piece_refs, acc_refs = refs[:count], refs[count:]
    for acc_ref in acc_refs:
        acc_ref[...] = jnp.zeros_like(acc_ref)

    def body(which, slot, col, block):
        both = product(dense_ref[col], piece_refs[which][slot * TB : (slot + 1) * TB, :])
        acc_refs[which][block] += both[:, :TB] + both[:, TB:]

    for_tiles(slots, piece_refs, body)


def first(dense, pieces, slots):
    return pl.pallas_call(
        functools.partial(first_kernel, slots),
        out_shape=[jax.ShapeDtypeStruct((RB, 2 * PANEL, TB), jnp.float32)] * len(pieces),
        in_specs=[VSPEC] * (1 + len(pieces)),
        out_specs=[VSPEC] * len(pieces),
        compiler_params=params(),
        cost_estimate=cost(1 << 25, 1 << 25),
        name="first",
    )(dense, *pieces)


def second_kernel(slots, dense_ref, acc_ref, piece_ref, kept_ref, other_ref, sum_ref):
    sum_ref[...] = acc_ref[...]

    def body(which, slot, col, block):
        both = product(dense_ref[col], piece_ref[slot * TB : (slot + 1) * TB, :])
        sum_ref[block] += both[:, :TB] + both[:, TB:]

    for_tiles(slots, (piece_ref,), body)
    for block in range(RB):
        lanes = slice(block * TB, (block + 1) * TB)
        kept_ref[:, lanes] = sum_ref[block, :PANEL, :]
        other_ref[:, lanes] = sum_ref[block, PANEL:, :]


def second(dense, acc, piece, slots):
    return pl.pallas_call(
        functools.partial(second_kernel, slots),
        out_shape=[jax.ShapeDtypeStruct((PANEL, PANEL), jnp.float32)] * 2,
        in_specs=[VSPEC] * 3,
        out_specs=[VSPEC] * 2,
        scratch_shapes=[pltpu.VMEM((RB, 2 * PANEL, TB), jnp.float32)],
        compiler_params=params(),
        cost_estimate=cost(1 << 25, 1 << 25),
        name="second",
    )(dense, acc, piece)


def join_kernel(same_own_ref, cross_own_ref, cross_far_ref, same_far_ref, out_hbm, out_ref, sems):
    core = lax.axis_index("rows") & 1
    start = pl.multiple_of(core * PANEL, PANEL)
    size = PANEL // STEPS
    copies = []
    for step in range(STEPS):
        rows = pl.ds(step * size, size)
        out_ref[rows, pl.ds(start, PANEL)] = same_own_ref[rows, :] + cross_far_ref[rows, :]
        out_ref[rows, pl.ds(PANEL - start, PANEL)] = same_far_ref[rows, :] + cross_own_ref[rows, :]
        copies.append(pltpu.make_async_copy(out_ref.at[rows], out_hbm.at[rows], sems.at[step]))
        copies[-1].start()
    for copy in copies:
        copy.wait()


def join(*results):
    shape = (PANEL, 2 * PANEL)
    return pl.pallas_call(
        join_kernel,
        out_shape=jax.ShapeDtypeStruct(shape, jnp.float32),
        in_specs=[VSPEC] * 4,
        out_specs=HSPEC,
        scratch_shapes=[pltpu.VMEM(shape, jnp.float32), pltpu.SemaphoreType.DMA((STEPS,))],
        compiler_params=params(),
        cost_estimate=cost(1 << 17, 1 << 17),
        name="join",
    )(*results)


def chunk(k, i, p):
    return k ^ p ^ (3 * (i ^ (p & 1) ^ (p >> 1)))


def pairs(place):
    out = []
    for row in range(8):
        for col in range(4):
            chip, core, plane = place(row >> 1, row & 1, col)
            out.append((row * 4 + col, (chip * 2 + core) * 4 + plane))
    return out


SWAP = pairs(lambda k, i, p: (k, 1 - i, p))
NEXT = pairs(lambda k, i, p: (k, i, p ^ 1))
SEND_SAME = pairs(lambda k, i, p: (chunk(k, i, p), i, p))
SEND_CROSS = pairs(lambda k, i, p: (chunk(k, 1 - i, p), 1 - i, p))
DONE_SAME = pairs(lambda k, i, p: (k, i, chunk(k, i, p)))
DONE_CROSS = pairs(lambda k, i, p: (k, 1 - i, chunk(k, i, p)))


def send(pieces, perms):
    return [lax.ppermute(piece, AXES, perm) for piece, perm in zip(pieces, perms)]


def after(x, *others):
    return lax.optimization_barrier((x, *others))[0]


def per_device(tiles, tile_rows, tile_cols, counts, scaling):
    slots = tiles.shape[1]
    own = pack(tiles, tile_rows, tile_cols, counts, scaling)
    near = lax.ppermute(own, AXES, NEXT)
    own_same, own_cross, own_other = send([own] * 3, (SEND_SAME, SEND_CROSS, SWAP))
    own_dense = spread(own, own_other, slots)
    near_other = lax.ppermute(after(near, own_dense), AXES, SWAP)
    near_dense = spread(near, near_other, slots)
    near_same, near_cross = send((after(near, own_same), after(near, own_cross)), (SEND_SAME, SEND_CROSS))
    accs = first(own_dense, (own_same, own_cross), slots)
    same, cross = [], []
    for acc, piece in zip(accs, (near_same, near_cross)):
        kept, other = second(near_dense, acc, piece, slots)
        same.append(lax.ppermute(kept, AXES, DONE_SAME))
        cross.append(lax.ppermute(other, AXES, DONE_CROSS))
    return join(same[0], cross[0], cross[1], same[1])


def densify(tile_set, row_ids, col_ids, live_mask, scale_set, block_count):
    placed = jnp.zeros((block_count, RB, TB, TB), jnp.float32)
    placed = placed.at[col_ids, row_ids].add(tile_set * live_mask[:, None, None])
    placed = placed * scale_set[:, None, None, :]
    return placed.reshape(block_count, RB * TB, TB)


def place_panels(blocked, tile_set, row_ids, col_ids, live_mask, panel_count):
    picked = jnp.take(blocked, col_ids, axis=0)
    product = jnp.einsum("kac,kbc->kab", picked, tile_set, precision=lax.Precision.HIGHEST)
    product = product.reshape(panel_count, -1, RB * TB, TB)
    hit_row = (row_ids[:, None] == jnp.arange(RB, dtype=jnp.int32)[None, :]).astype(
        jnp.float32
    ) * live_mask[:, None]
    hit_row = hit_row.reshape(panel_count, -1, RB)
    placed = jnp.einsum("pkr,pkab->aprb", hit_row, product, precision=lax.Precision.HIGHEST)
    return placed.reshape(RB * TB, panel_count * RB * TB)


def per_device_any(tiles, tile_rows, tile_cols, counts, scaling):
    slot_total = tiles.shape[1]
    slot_range = jnp.arange(slot_total, dtype=jnp.int32)
    own_live = (slot_range < counts[0, 0]).astype(jnp.float32)
    blocked = densify(
        tiles[0], tile_rows[0], tile_cols[0], own_live, scaling.reshape(CB_DEV, TB), CB_DEV
    )
    piece_tiles = lax.all_gather(tiles, "rows", axis=0, tiled=True)
    piece_rows = lax.all_gather(tile_rows, "rows", axis=0, tiled=True)
    piece_cols = lax.all_gather(tile_cols, "rows", axis=0, tiled=True)
    piece_counts = lax.all_gather(counts, "rows", axis=0, tiled=True)
    count_here = piece_tiles.shape[0]
    live_mask = (slot_range[None, :] < piece_counts).astype(jnp.float32).reshape(-1)
    tile_block = place_panels(
        blocked,
        piece_tiles.reshape(count_here * slot_total, TB, TB),
        piece_rows.reshape(-1),
        piece_cols.reshape(-1),
        live_mask,
        count_here,
    )
    return lax.psum_scatter(tile_block, "cols", scatter_dimension=1, tiled=True)


def solution(mesh):
    placed = (
        P("rows", "cols", None, None),
        P("rows", "cols"),
        P("rows", "cols"),
        P("rows", "cols"),
        P("cols"),
    )
    small = mesh.shape["rows"] == 8 and mesh.shape["cols"] == 4
    return jax.shard_map(
        per_device if small else per_device_any,
        mesh=mesh,
        in_specs=placed,
        out_specs=P("rows", "cols"),
        check_vma=False,
    )
```
